32 devices in a mesh: prod: 8 (over y, x, core), pre: 4 (over z).
Axes of the slice: x: 2, y: 2, z: 4, core: 2. Of those that a mesh axis runs over, the one named last changes fastest.
Arguments:
- potentials: bfloat16 [128, 16, 512], P(('prod', 'pre')), may hold values from -6 to 6
- injected: float32 [128, 16, 512], P(('prod', 'pre')), may hold values from -6 to 6
- near_blocks: bfloat16 [128, 4, 512, 512], P('prod', 'pre'), may hold values from -0.125 to 0.125
- near_cols: int32 [128, 4], P('prod', 'pre'), may hold values from 0 to 127, as said below
- row_basis: bfloat16 [128, 16, 512], P('prod'), may hold values from -1.5 to 1.5
- col_basis: bfloat16 [128, 16, 512], P(('prod', 'pre')), may hold values from -0.25 to 0.25
- basis_ranks: int32 [128], P(('prod', 'pre')), may hold values from 1 to 16
- couplings: bfloat16 [128, 16, 2048], P('prod', None, 'pre'), may hold values from -0.125 to 0.125
- inverses: bfloat16 [128, 512, 512], P(('prod', 'pre')), may hold values from -0.25 to 0.25
Outputs:
- residual: float32 [128, 16, 512], P(('prod', 'pre'))
- corrected: float32 [128, 16, 512], P(('prod', 'pre'))
The draws below stay inside these ranges and needn't reach their ends.
Inputs may be any that keep to these rules, and one draw needn't show every extreme that they name: near_cols[i, 0] = i; near_cols[i, 1] is i + 8 or i - 8; every other entry differs from i by 1 to 7.
All inputs are finite; a program needn't handle non-finite values.
Results may differ from the reference program's by a relative error of at most 0.012.
Values may be sent and summed in bfloat16 or wider, within the bound.
A program may use at most 64 MiB of HBM per device.

```python
import jax
import jax.numpy as jnp
from jax import lax

P_SIZE = 512
K = 16
S = 16
NC = 128
CPD = 4
BAND = 8
NB = 4
N_PROD = 8
N_PRE = 4


def draw_near_cols(key, part):
    first_key, second_key = jax.random.split(key)
    row_ids = jnp.arange(NC, dtype=jnp.int32)
    signs = jax.random.randint(first_key, (NC,), 0, 2).astype(jnp.int32) * 2 - 1
    steps_up = jnp.arange(1, BAND, dtype=jnp.int32)
    candidates = jnp.concatenate([steps_up, -steps_up])
    row_keys = jax.random.split(second_key, NC)
    shuffled = jax.vmap(lambda one_key: jax.random.permutation(one_key, candidates))(row_keys)[:, :NB - 2]
    offsets = jnp.concatenate([jnp.zeros((NC, 1), jnp.int32), (signs * BAND)[:, None], shuffled.astype(jnp.int32)], axis=1)
    columns = row_ids[:, None] + offsets
    outside = (columns < 0) | (columns >= NC)
    return jnp.where(outside, row_ids[:, None] - offsets, columns).astype(jnp.int32)


def touch_ends(values, stream_key, smallest, high):
    shape = values.shape
    spot = [jax.random.randint(jax.random.fold_in(stream_key, axis), (), 0, shape[axis]) for axis in range(len(shape))]
    values = values.at[tuple(spot)].set(smallest)
    longest = shape.index(max(shape))
    spot[longest] = (spot[longest] + 1) % shape[longest]
    return values.at[tuple(spot)].set(high)


def level_of(stream_key, shape, shards, smallest, high):
    loudness, own = 1.0, jax.random.fold_in(stream_key, 6)
    for position, parts in shards:
        steps = jnp.exp(jax.random.uniform(jax.random.fold_in(own, position), (parts,), jnp.float32, smallest / len(shards), high / len(shards)))
        loudness = loudness * jnp.repeat(steps, shape[position] // parts).reshape([-1 if axis == position else 1 for axis in range(len(shape))])
    return loudness


def centred(stream_key, dims, scale, most, pieces=(), kind=jnp.bfloat16):
    array = jax.random.normal(stream_key, dims, jnp.float32) * scale
    if len(pieces) > 0:
        array = level_of(stream_key, dims, pieces, -0.22, 0.18) * array
    return jnp.clip(array, min=-most, max=most).astype(kind)


def setup_inputs(seed: int = 0) -> dict:
    keys = jax.random.split(jax.random.key(seed), 10)
    potentials = centred(keys[0], (NC, S, P_SIZE), 1.0, 6.0, ((0, 32),))
    injected = centred(keys[1], (NC, S, P_SIZE), 1.0, 6.0, ((0, 32),), jnp.float32)
    near_blocks = centred(keys[2], (NC, NB, P_SIZE, P_SIZE), (NB * P_SIZE) ** -0.5, 0.125, ((0, 8), (1, 4)))
    near_cols = draw_near_cols(jax.random.fold_in(keys[9], 71), 0)
    row_basis = centred(keys[4], (NC, K, P_SIZE), K ** -0.5, 1.5, ((0, 8),))
    col_basis = centred(keys[5], (NC, K, P_SIZE), P_SIZE ** -0.5, 0.25, ((0, 32),))
    basis_ranks = touch_ends(jax.random.randint(keys[6], (NC,), 1, K + 1), jax.random.fold_in(keys[6], 1), 1, K).astype(jnp.int32)
    couplings = centred(keys[7], (NC, K, NC * K), (NC * K) ** -0.5, 0.125, ((0, 8), (2, 4)))
    inverses = centred(keys[8], (NC, P_SIZE, P_SIZE), P_SIZE ** -0.5, 0.25, ((0, 32),))
    return {"potentials": potentials, "injected": injected, "near_blocks": near_blocks, "near_cols": near_cols, "row_basis": row_basis, "col_basis": col_basis, "basis_ranks": basis_ranks, "couplings": couplings, "inverses": inverses}


def reference(potentials, injected, near_blocks, near_cols, row_basis, col_basis, basis_ranks, couplings, inverses):
    coeffs = lax.dot_general(potentials, col_basis, (((2,), (2,)), ((0,), (0,))), preferred_element_type=jnp.float32)
    levels = jnp.arange(K, dtype=jnp.int32)[None, :]
    kept_levels = levels < basis_ranks[:, None]
    coeffs = jnp.where(kept_levels[:, None, :], coeffs, jnp.zeros_like(coeffs)).astype(jnp.bfloat16)
    ordered = coeffs.reshape(N_PROD, N_PRE, CPD, S, K).transpose(1, 0, 2, 4, 3).reshape(NC * K, S)
    weights = jnp.dot(couplings.reshape(NC * K, NC * K), ordered, preferred_element_type=jnp.float32)
    weights = weights.reshape(NC, K, S).astype(jnp.bfloat16)
    far_field = lax.dot_general(weights, row_basis, (((1,), (1,)), ((0,), (0,))), preferred_element_type=jnp.float32)

    def near_row(block_pair):
        blocks, columns = block_pair
        picked = potentials[columns]
        return lax.dot_general(picked, blocks, (((0, 2), (0, 2)), ((), ())), preferred_element_type=jnp.float32)

    near_field = lax.map(near_row, (near_blocks, near_cols))
    residual = injected - (near_field + far_field)
    halfway = residual.astype(jnp.bfloat16)
    corrected = lax.dot_general(halfway, inverses, (((2,), (2,)), ((0,), (0,))), preferred_element_type=jnp.float32)
    return residual, corrected
```

```python
import functools

import jax
import jax.numpy as jnp
from jax import lax
from jax.experimental import pallas as pl
from jax.experimental.pallas import tpu as pltpu
from jax.sharding import PartitionSpec as P

MESH = pl.DeviceIdType.MESH
NT = (((1,), (1,)), ((), ()))


def kernel(
    n_prod,
    n_pre,
    pot_hbm,
    inj_hbm,
    near_hbm,
    cols_ref,
    rowb_hbm,
    colb_hbm,
    ranks_ref,
    coup_hbm,
    inv_hbm,
    res_ref,
    cor_ref,
    band,
    inj,
    near,
    rowb,
    colb,
    coup,
    inv,
    coef,
    far,
    mine,
    sending,
    arriving,
    load_sem,
    near_sem,
    gather_send,
    gather_recv,
    halo_send,
    halo_recv,
    coef_send,
    coef_recv,
    part_send,
    part_recv,
):
    owned, scen, panels = pot_hbm.shape
    rows = near_hbm.shape[0]
    rank_cap = colb_hbm.shape[1]
    half_rows = rows // 2
    half = n_pre // 2
    width = owned * rank_cap
    p = lax.axis_index("prod")
    z = lax.axis_index("pre")
    high, low = z // half, z % half
    others = [(1 - high) * half + (low + e) % half for e in range(half)]
    others += [high * half + (low + e) % half for e in range(1, half)]
    nearest = others[half:] + others[:half]

    def slot(first):
        return band.at[pl.ds(first, owned)]

    own = half_rows + z * owned
    load_pot = pltpu.make_async_copy(pot_hbm, slot(own), load_sem.at[0])
    load_colb = pltpu.make_async_copy(colb_hbm, colb, load_sem.at[1])
    load_coup = pltpu.make_async_copy(coup_hbm, coup, load_sem.at[2])
    load_rowb = pltpu.make_async_copy(rowb_hbm, rowb, load_sem.at[3])
    load_inj = pltpu.make_async_copy(inj_hbm, inj, load_sem.at[4])
    load_inv = pltpu.make_async_copy(inv_hbm, inv, load_sem.at[5])
    load_pot.start()
    load_colb.start()

    barrier = pltpu.get_barrier_semaphore()
    for target in others:
        pl.semaphore_signal(barrier, inc=1, device_id=(p, target), device_id_type=MESH)
    for e in range(1, n_prod):
        pl.semaphore_signal(
            barrier, inc=1, device_id=((p + e) % n_prod, z), device_id_type=MESH
        )
    load_coup.start()
    load_rowb.start()
    near_loads = []
    for step, target in enumerate(others + [z]):
        near_loads.append(
            pltpu.make_async_copy(
                near_hbm.at[pl.ds(target * owned, owned), 0],
                near.at[pl.ds(target * owned, owned)],
                near_sem.at[step],
            )
        )
        near_loads[-1].start()
    load_inj.start()
    load_inv.start()
    load_pot.wait()
    load_colb.wait()
    pl.semaphore_wait(barrier, n_pre - 1 + n_prod - 1)

    gathers = []
    for e, target in enumerate(others):
        gathers.append(
            pltpu.make_async_remote_copy(
                src_ref=slot(own),
                dst_ref=slot(own),
                send_sem=gather_send.at[e],
                recv_sem=gather_recv.at[z],
                device_id=(p, target),
                device_id_type=MESH,
            )
        )
        gathers[-1].start()

    halos = []

    def forward(zs, index):
        lower = zs < half
        to = jnp.where(lower, p - 1, p + 1)
        first = half_rows + zs * owned
        there = jnp.where(lower, first + rows, first - rows)
        ok = (z >= 1) & (to >= 0) & (to < n_prod)
        copy = pltpu.make_async_remote_copy(
            src_ref=slot(first),
            dst_ref=slot(there),
            send_sem=halo_send.at[index],
            recv_sem=halo_recv.at[zs],
            device_id=(to, z),
            device_id_type=MESH,
        )

        @pl.when(ok)
        def _():
            copy.start()

        halos.append((ok, copy))

    forward(z, 0)

    pot = band[pl.ds(own, owned)].reshape(owned * scen, panels)
    basis = colb[...].reshape(width, panels)
    products = lax.dot_general(
        pot,
        jnp.concatenate([basis] * (128 // width), axis=0),
        NT,
        preferred_element_type=jnp.float32,
    )
    lane = lax.broadcasted_iota(jnp.int32, (scen, 128), 1)
    inner = lane % width
    here = (lane // width) == p % (128 // width)
    mine_coef = jnp.zeros((scen, 128), jnp.float32)
    for j in range(owned):
        keep = here & (inner // rank_cap == j) & (inner % rank_cap < ranks_ref[j])
        mine_coef = jnp.where(keep, products[j * scen : (j + 1) * scen], mine_coef)
    coef[p] = mine_coef.astype(jnp.bfloat16)
    coef_copies = []
    for e in range(1, n_prod):
        coef_copies.append(
            pltpu.make_async_remote_copy(
                src_ref=coef.at[p],
                dst_ref=coef.at[p],
                send_sem=coef_send.at[e],
                recv_sem=coef_recv.at[p],
                device_id=((p + e) % n_prod, z),
                device_id_type=MESH,
            )
        )
        coef_copies[-1].start()

    for index, zs in enumerate(nearest):
        pltpu.make_async_remote_copy(
            src_ref=slot(half_rows + zs * owned),
            dst_ref=slot(half_rows + zs * owned),
            send_sem=gather_send.at[0],
            recv_sem=gather_recv.at[zs],
            device_id=(p, zs),
            device_id_type=MESH,
        ).wait_recv()
        forward(zs, index + 1)

    for e in range(1, n_prod):
        b = (p + e) % n_prod
        pltpu.make_async_remote_copy(
            src_ref=coef.at[b],
            dst_ref=coef.at[b],
            send_sem=coef_send.at[0],
            recv_sem=coef_recv.at[b],
            device_id=(b, z),
            device_id_type=MESH,
        ).wait_recv()
    load_coup.wait()
    load_rowb.wait()
    share = 128 // width
    blocks = []
    for m in range(n_prod // share):
        block = coef[m * share]
        for e in range(1, share):
            block = block + coef[m * share + e]
        blocks.append(block)
    columns = jnp.concatenate(blocks, axis=1)
    weights = lax.dot_general(
        columns,
        coup[...].reshape(rows * rank_cap, n_prod * width),
        NT,
        preferred_element_type=jnp.float32,
    )
    weights = jnp.concatenate([weights] * rows, axis=0)
    shape = (rows * scen, rows * rank_cap)
    row_of = lax.broadcasted_iota(jnp.int32, shape, 0) // scen
    col_of = lax.broadcasted_iota(jnp.int32, shape, 1) // rank_cap
    weights = jnp.where(row_of == col_of, weights, 0.0).astype(jnp.bfloat16)
    far[...] = jnp.dot(
        weights,
        rowb[...].reshape(rows * rank_cap, panels),
        preferred_element_type=jnp.float32,
    ).reshape(rows, scen, panels)

    for zs in range(n_pre):
        source = p + 1 if zs < half else p - 1
        first = half_rows + zs * owned + (rows if zs < half else -rows)

        @pl.when((z >= 1) & (source >= 0) & (source < n_prod))
        def _():
            pltpu.make_async_remote_copy(
                src_ref=slot(first),
                dst_ref=slot(first),
                send_sem=halo_send.at[0],
                recv_sem=halo_recv.at[zs],
                device_id=(source, z),
                device_id_type=MESH,
            ).wait_recv()

    offset = p * rows - half_rows

    def partial_row(row):
        picked = band[jnp.clip(cols_ref[row] - offset, 0, 2 * rows - 1)]
        value = lax.dot_general(picked, near[row], NT, preferred_element_type=jnp.float32)
        return value + far[row]

    parts = []
    for e, target in enumerate(others):
        near_loads[e].wait()
        for j in range(owned):
            row = target * owned + j
            sending[e, j] = partial_row(row).astype(jnp.bfloat16)
        parts.append(
            pltpu.make_async_remote_copy(
                src_ref=sending.at[e],
                dst_ref=arriving.at[z],
                send_sem=part_send.at[e],
                recv_sem=part_recv.at[z],
                device_id=(p, target),
                device_id_type=MESH,
            )
        )
        parts[-1].start()
    near_loads[-1].wait()
    load_inj.wait()
    for j in range(owned):
        mine[j] = inj[j] - partial_row(z * owned + j)
    load_inv.wait()
    for zs in nearest:
        pltpu.make_async_remote_copy(
            src_ref=arriving.at[zs],
            dst_ref=arriving.at[zs],
            send_sem=part_send.at[0],
            recv_sem=part_recv.at[zs],
            device_id=(p, zs),
            device_id_type=MESH,
        ).wait_recv()
    for j in range(owned):
        summed = arriving[others[0], j].astype(jnp.float32)
        for zs in others[1:]:
            summed = summed + arriving[zs, j].astype(jnp.float32)
        residual = mine[j] - summed
        res_ref[j] = residual
        cor_ref[j] = lax.dot_general(
            residual.astype(jnp.bfloat16), inv[j], NT, preferred_element_type=jnp.float32
        )
    for copy in gathers + coef_copies + parts:
        copy.wait_send()
    for ok, copy in halos:

        @pl.when(ok)
        def _():
            copy.wait_send()


def local(n_prod, n_pre, potentials, injected, near, cols, rowb, colb, ranks, coup, inv):
    owned, scen, panels = potentials.shape
    rows = near.shape[0]
    out = jax.ShapeDtypeStruct(injected.shape, jnp.float32)
    anywhere = pl.BlockSpec(memory_space=pltpu.HBM)
    scalars = pl.BlockSpec(memory_space=pltpu.SMEM)
    vmem = pl.BlockSpec(memory_space=pltpu.VMEM)
    dma = pltpu.SemaphoreType.DMA
    blocks = rows + owned
    return pl.pallas_call(
        functools.partial(kernel, n_prod, n_pre),
        out_shape=(out, out),
        in_specs=[
            anywhere,
            anywhere,
            anywhere,
            scalars,
            anywhere,
            anywhere,
            scalars,
            anywhere,
            anywhere,
        ],
        out_specs=(vmem, vmem),
        scratch_shapes=[
            pltpu.VMEM((2 * rows, scen, panels), jnp.bfloat16),
            pltpu.VMEM(injected.shape, jnp.float32),
            pltpu.VMEM((rows, panels, panels), jnp.bfloat16),
            pltpu.VMEM(rowb.shape, jnp.bfloat16),
            pltpu.VMEM(colb.shape, jnp.bfloat16),
            pltpu.VMEM(coup.shape, jnp.bfloat16),
            pltpu.VMEM(inv.shape, jnp.bfloat16),
            pltpu.VMEM((n_prod, scen, 128), jnp.bfloat16),
            pltpu.VMEM((rows, scen, panels), jnp.float32),
            pltpu.VMEM(injected.shape, jnp.float32),
            pltpu.VMEM((n_pre - 1, owned, scen, panels), jnp.bfloat16),
            pltpu.VMEM((n_pre, owned, scen, panels), jnp.bfloat16),
            dma((6,)),
            dma((n_pre,)),
            dma((n_pre,)),
            dma((n_pre,)),
            dma((n_pre,)),
            dma((n_pre,)),
            dma((n_prod,)),
            dma((n_prod,)),
            dma((n_pre,)),
            dma((n_pre,)),
        ],
        compiler_params=pltpu.CompilerParams(
            collective_id=0, has_side_effects=True, vmem_limit_bytes=63 * 2**20
        ),
        cost_estimate=pl.CostEstimate(
            flops=2 * blocks * scen * panels * panels,
            bytes_accessed=2 * blocks * panels * panels,
            transcendentals=0,
        ),
    )(potentials, injected, near, cols.reshape(rows), rowb, colb, ranks, coup, inv)


def solution(mesh):
    return jax.shard_map(
        functools.partial(local, mesh.shape["prod"], mesh.shape["pre"]),
        mesh=mesh,
        in_specs=(
            P(("prod", "pre"), None, None),
            P(("prod", "pre"), None, None),
            P("prod", "pre", None, None),
            P("prod", "pre"),
            P("prod", None, None),
            P(("prod", "pre"), None, None),
            P(("prod", "pre")),
            P("prod", None, "pre"),
            P(("prod", "pre"), None, None),
        ),
        out_specs=(P(("prod", "pre"), None, None), P(("prod", "pre"), None, None)),
        check_vma=False,
    )
```

```python
import functools

import jax
import jax.numpy as jnp
from jax import lax
from jax.experimental import pallas as pl
from jax.experimental.pallas import tpu as pltpu
from jax.sharding import PartitionSpec as P

MESH = pl.DeviceIdType.MESH
NT = (((1,), (1,)), ((), ()))


def kernel(
    n_prod,
    n_pre,
    pot_hbm,
    inj_hbm,
    near_hbm,
    cols_ref,
    rowb_hbm,
    colb_hbm,
    ranks_ref,
    coup_hbm,
    inv_hbm,
    res_ref,
    cor_ref,
    band,
    inj,
    near,
    rowb,
    colb,
    coup,
    inv,
    coef,
    far,
    mine,
    res,
    cor,
    sending,
    arriving,
    load_sem,
    near_sem,
    gather_send,
    gather_recv,
    halo_send,
    halo_recv,
    coef_send,
    coef_recv,
    part_send,
    part_recv,
    out_sem,
):
    owned, scen, panels = pot_hbm.shape
    rows = near_hbm.shape[0]
    rank_cap = colb_hbm.shape[1]
    half_rows = rows // 2
    half = n_pre // 2
    width = owned * rank_cap
    p = lax.axis_index("prod")
    z = lax.axis_index("pre")
    high, low = z // half, z % half
    others = [(1 - high) * half + (low + e) % half for e in range(half)]
    others += [high * half + (low + e) % half for e in range(1, half)]
    nearest = others[half:] + others[:half]

    def slot(first):
        return band.at[pl.ds(first, owned)]

    own = half_rows + z * owned
    load_pot = pltpu.make_async_copy(pot_hbm, slot(own), load_sem.at[0])
    load_colb = pltpu.make_async_copy(colb_hbm, colb, load_sem.at[1])
    load_coup = pltpu.make_async_copy(coup_hbm, coup, load_sem.at[2])
    load_rowb = pltpu.make_async_copy(rowb_hbm, rowb, load_sem.at[3])
    load_inj = pltpu.make_async_copy(inj_hbm, inj, load_sem.at[4])
    load_inv = pltpu.make_async_copy(inv_hbm, inv, load_sem.at[5])
    load_pot.start()
    load_colb.start()

    barrier = pltpu.get_barrier_semaphore()
    for target in others:
        pl.semaphore_signal(barrier, inc=1, device_id=(p, target), device_id_type=MESH)
    for e in range(1, n_prod):
        pl.semaphore_signal(
            barrier, inc=1, device_id=((p + e) % n_prod, z), device_id_type=MESH
        )
    pl.semaphore_wait(barrier, n_pre - 1 + n_prod - 1)

    gathers = []
    for e, target in enumerate(others):
        gathers.append(
            pltpu.make_async_remote_copy(
                src_ref=pot_hbm,
                dst_ref=slot(own),
                send_sem=gather_send.at[e],
                recv_sem=gather_recv.at[z],
                device_id=(p, target),
                device_id_type=MESH,
            )
        )
        gathers[-1].start()

    halos = []

    def forward(zs, index, source=None):
        lower = zs < half
        to = jnp.where(lower, p - 1, p + 1)
        first = half_rows + zs * owned
        there = jnp.where(lower, first + rows, first - rows)
        ok = (z >= 1) & (to >= 0) & (to < n_prod)
        copy = pltpu.make_async_remote_copy(
            src_ref=slot(first) if source is None else source,
            dst_ref=slot(there),
            send_sem=halo_send.at[index],
            recv_sem=halo_recv.at[zs],
            device_id=(to, z),
            device_id_type=MESH,
        )

        @pl.when(ok)
        def _():
            copy.start()

        halos.append((ok, copy))

    forward(z, 0, pot_hbm)
    load_coup.start()
    load_rowb.start()
    order = [(target, j) for j in range(owned) for target in others]
    order += [(z, j) for j in range(owned)]
    near_loads = []
    for step, (target, j) in enumerate(order):
        row = target * owned + j
        near_loads.append(
            pltpu.make_async_copy(near_hbm.at[row, 0], near.at[row], near_sem.at[step])
        )
        near_loads[-1].start()
    load_inj.start()
    load_inv.start()
    load_pot.wait()
    load_colb.wait()

    pot = band[pl.ds(own, owned)].reshape(owned * scen, panels)
    basis = colb[...].reshape(width, panels)
    products = lax.dot_general(
        pot,
        jnp.concatenate([basis] * (128 // width), axis=0),
        NT,
        preferred_element_type=jnp.float32,
    )
    lane = lax.broadcasted_iota(jnp.int32, (scen, 128), 1)
    inner = lane % width
    here = (lane // width) == p % (128 // width)
    mine_coef = jnp.zeros((scen, 128), jnp.float32)
    for j in range(owned):
        keep = here & (inner // rank_cap == j) & (inner % rank_cap < ranks_ref[j])
        mine_coef = jnp.where(keep, products[j * scen : (j + 1) * scen], mine_coef)
    coef[p] = mine_coef.astype(jnp.bfloat16)
    coef_copies = []
    for e in range(1, n_prod):
        coef_copies.append(
            pltpu.make_async_remote_copy(
                src_ref=coef.at[p],
                dst_ref=coef.at[p],
                send_sem=coef_send.at[e],
                recv_sem=coef_recv.at[p],
                device_id=((p + e) % n_prod, z),
                device_id_type=MESH,
            )
        )
        coef_copies[-1].start()

    def collect(index):
        zs = nearest[index]
        pltpu.make_async_remote_copy(
            src_ref=slot(half_rows + zs * owned),
            dst_ref=slot(half_rows + zs * owned),
            send_sem=gather_send.at[0],
            recv_sem=gather_recv.at[zs],
            device_id=(p, zs),
            device_id_type=MESH,
        ).wait_recv()
        forward(zs, index + 1)

    collect(0)

    for e in range(1, n_prod):
        b = (p + e) % n_prod
        pltpu.make_async_remote_copy(
            src_ref=coef.at[b],
            dst_ref=coef.at[b],
            send_sem=coef_send.at[0],
            recv_sem=coef_recv.at[b],
            device_id=(b, z),
            device_id_type=MESH,
        ).wait_recv()
    load_coup.wait()
    load_rowb.wait()
    share = 128 // width
    blocks = []
    for m in range(n_prod // share):
        block = coef[m * share]
        for e in range(1, share):
            block = block + coef[m * share + e]
        blocks.append(block)
    columns = jnp.concatenate(blocks, axis=1)
    weights = lax.dot_general(
        columns,
        coup[...].reshape(rows * rank_cap, n_prod * width),
        NT,
        preferred_element_type=jnp.float32,
    )
    weights = jnp.concatenate([weights] * rows, axis=0)
    shape = (rows * scen, rows * rank_cap)
    row_of = lax.broadcasted_iota(jnp.int32, shape, 0) // scen
    col_of = lax.broadcasted_iota(jnp.int32, shape, 1) // rank_cap
    weights = jnp.where(row_of == col_of, weights, 0.0).astype(jnp.bfloat16)
    far[...] = jnp.dot(
        weights,
        rowb[...].reshape(rows * rank_cap, panels),
        preferred_element_type=jnp.float32,
    ).reshape(rows, scen, panels)

    for index in range(1, n_pre - 1):
        collect(index)

    for zs in range(n_pre):
        source = p + 1 if zs < half else p - 1
        first = half_rows + zs * owned + (rows if zs < half else -rows)

        @pl.when((z >= 1) & (source >= 0) & (source < n_prod))
        def _():
            pltpu.make_async_remote_copy(
                src_ref=slot(first),
                dst_ref=slot(first),
                send_sem=halo_send.at[0],
                recv_sem=halo_recv.at[zs],
                device_id=(source, z),
                device_id_type=MESH,
            ).wait_recv()

    offset = p * rows - half_rows

    def partial_row(row):
        picked = band[jnp.clip(cols_ref[row] - offset, 0, 2 * rows - 1)]
        value = lax.dot_general(picked, near[row], NT, preferred_element_type=jnp.float32)
        return value + far[row]

    parts = []
    for step, (target, j) in enumerate(order[: -owned]):
        near_loads[step].wait()
        sending[step] = partial_row(target * owned + j).astype(jnp.bfloat16)
        parts.append(
            pltpu.make_async_remote_copy(
                src_ref=sending.at[step],
                dst_ref=arriving.at[z, j],
                send_sem=part_send.at[step],
                recv_sem=part_recv.at[z, j],
                device_id=(p, target),
                device_id_type=MESH,
            )
        )
        parts[-1].start()
    load_inj.wait()
    for j in range(owned):
        near_loads[len(parts) + j].wait()
        mine[j] = inj[j] - partial_row(z * owned + j)
    load_inv.wait()
    writes = []
    for j in range(owned):
        residual = mine[j]
        for zs in nearest:
            pltpu.make_async_remote_copy(
                src_ref=arriving.at[zs, j],
                dst_ref=arriving.at[zs, j],
                send_sem=part_send.at[0],
                recv_sem=part_recv.at[zs, j],
                device_id=(p, zs),
                device_id_type=MESH,
            ).wait_recv()
            residual = residual - arriving[zs, j].astype(jnp.float32)
        res[j] = residual
        writes.append(pltpu.make_async_copy(res.at[j], res_ref.at[j], out_sem.at[0, j]))
        writes[-1].start()
        cor[j] = lax.dot_general(
            residual.astype(jnp.bfloat16), inv[j], NT, preferred_element_type=jnp.float32
        )
        writes.append(pltpu.make_async_copy(cor.at[j], cor_ref.at[j], out_sem.at[1, j]))
        writes[-1].start()
    for copy in writes:
        copy.wait()
    for copy in gathers + coef_copies + parts:
        copy.wait_send()
    for ok, copy in halos:

        @pl.when(ok)
        def _():
            copy.wait_send()


def hand_over(res_in, cor_in, res_out, cor_out, sem):
    first = pltpu.make_async_copy(res_in, res_out, sem.at[0])
    second = pltpu.make_async_copy(cor_in, cor_out, sem.at[1])
    first.start()
    second.start()
    first.wait()
    second.wait()


def local(n_prod, n_pre, potentials, injected, near, cols, rowb, colb, ranks, coup, inv):
    owned, scen, panels = potentials.shape
    rows = near.shape[0]
    out = jax.ShapeDtypeStruct(injected.shape, jnp.float32)
    anywhere = pl.BlockSpec(memory_space=pltpu.HBM)
    scalars = pl.BlockSpec(memory_space=pltpu.SMEM)
    dma = pltpu.SemaphoreType.DMA
    blocks = rows + owned
    residual, corrected = pl.pallas_call(
        functools.partial(kernel, n_prod, n_pre),
        out_shape=(out, out),
        in_specs=[
            anywhere,
            anywhere,
            anywhere,
            scalars,
            anywhere,
            anywhere,
            scalars,
            anywhere,
            anywhere,
        ],
        out_specs=(anywhere, anywhere),
        scratch_shapes=[
            pltpu.VMEM((2 * rows, scen, panels), jnp.bfloat16),
            pltpu.VMEM(injected.shape, jnp.float32),
            pltpu.VMEM((rows, panels, panels), jnp.bfloat16),
            pltpu.VMEM(rowb.shape, jnp.bfloat16),
            pltpu.VMEM(colb.shape, jnp.bfloat16),
            pltpu.VMEM(coup.shape, jnp.bfloat16),
            pltpu.VMEM(inv.shape, jnp.bfloat16),
            pltpu.VMEM((n_prod, scen, 128), jnp.bfloat16),
            pltpu.VMEM((rows, scen, panels), jnp.float32),
            pltpu.VMEM(injected.shape, jnp.float32),
            pltpu.VMEM(injected.shape, jnp.float32),
            pltpu.VMEM(injected.shape, jnp.float32),
            pltpu.VMEM(((n_pre - 1) * owned, scen, panels), jnp.bfloat16),
            pltpu.VMEM((n_pre, owned, scen, panels), jnp.bfloat16),
            dma((6,)),
            dma((rows,)),
            dma((n_pre,)),
            dma((n_pre,)),
            dma((n_pre,)),
            dma((n_pre,)),
            dma((n_prod,)),
            dma((n_prod,)),
            dma(((n_pre - 1) * owned,)),
            dma((n_pre, owned)),
            dma((2, owned)),
        ],
        compiler_params=pltpu.CompilerParams(
            collective_id=0, has_side_effects=True, vmem_limit_bytes=63 * 2**20
        ),
        cost_estimate=pl.CostEstimate(
            flops=2 * blocks * scen * panels * panels,
            bytes_accessed=2 * blocks * panels * panels,
            transcendentals=0,
        ),
    )(potentials, injected, near, cols.reshape(rows), rowb, colb, ranks, coup, inv)
    return pl.pallas_call(
        hand_over,
        out_shape=(out, out),
        in_specs=[anywhere, anywhere],
        out_specs=(anywhere, anywhere),
        scratch_shapes=[dma((2,))],
        compiler_params=pltpu.CompilerParams(vmem_limit_bytes=63 * 2**20),
    )(residual, corrected)


def solution(mesh):
    return jax.shard_map(
        functools.partial(local, mesh.shape["prod"], mesh.shape["pre"]),
        mesh=mesh,
        in_specs=(
            P(("prod", "pre"), None, None),
            P(("prod", "pre"), None, None),
            P("prod", "pre", None, None),
            P("prod", "pre"),
            P("prod", None, None),
            P(("prod", "pre"), None, None),
            P(("prod", "pre")),
            P("prod", None, "pre"),
            P(("prod", "pre"), None, None),
        ),
        out_specs=(P(("prod", "pre"), None, None), P(("prod", "pre"), None, None)),
        check_vma=False,
    )
```

```python
import functools

import jax
import jax.numpy as jnp
from jax import lax
from jax.experimental import pallas as pl
from jax.experimental.pallas import tpu as pltpu
from jax.sharding import PartitionSpec as P

MESH = pl.DeviceIdType.MESH
NT = (((1,), (1,)), ((), ()))


def kernel(
    n_prod,
    n_pre,
    pot_hbm,
    inj_hbm,
    near_hbm,
    cols_ref,
    rowb_hbm,
    colb_hbm,
    ranks_ref,
    coup_hbm,
    inv_hbm,
    res_ref,
    cor_ref,
    band,
    inj,
    near,
    rowb,
    colb,
    coup,
    inv,
    coef,
    far,
    mine,
    res,
    cor,
    sending,
    arriving,
    load_sem,
    near_sem,
    gather_send,
    gather_recv,
    halo_send,
    halo_recv,
    coef_send,
    coef_recv,
    part_send,
    part_recv,
    out_sem,
):
    owned, scen, panels = pot_hbm.shape
    rows = near_hbm.shape[0]
    rank_cap = colb_hbm.shape[1]
    half_rows = rows // 2
    half = n_pre // 2
    width = owned * rank_cap
    p = lax.axis_index("prod")
    z = lax.axis_index("pre")
    high, low = z // half, z % half
    others = [(1 - high) * half + (low + e) % half for e in range(half)]
    others += [high * half + (low + e) % half for e in range(1, half)]
    nearest = others[half:] + others[:half]

    def slot(first):
        return band.at[pl.ds(first, owned)]

    own = half_rows + z * owned
    load_pot = pltpu.make_async_copy(pot_hbm, slot(own), load_sem.at[0])
    load_colb = pltpu.make_async_copy(colb_hbm, colb, load_sem.at[1])
    load_coup = pltpu.make_async_copy(coup_hbm, coup, load_sem.at[2])
    load_rowb = pltpu.make_async_copy(rowb_hbm, rowb, load_sem.at[3])
    load_inj = pltpu.make_async_copy(inj_hbm, inj, load_sem.at[4])
    load_inv = pltpu.make_async_copy(inv_hbm, inv, load_sem.at[5])
    load_pot.start()
    load_colb.start()

    barrier = pltpu.get_barrier_semaphore()
    for target in others:
        pl.semaphore_signal(barrier, inc=1, device_id=(p, target), device_id_type=MESH)
    for e in range(1, n_prod):
        pl.semaphore_signal(
            barrier, inc=1, device_id=((p + e) % n_prod, z), device_id_type=MESH
        )
    pl.semaphore_wait(barrier, n_pre - 1 + n_prod - 1)

    gathers = []
    for e, target in enumerate(others):
        gathers.append(
            pltpu.make_async_remote_copy(
                src_ref=pot_hbm,
                dst_ref=slot(own),
                send_sem=gather_send.at[e],
                recv_sem=gather_recv.at[z],
                device_id=(p, target),
                device_id_type=MESH,
            )
        )
        gathers[-1].start()

    halos = []

    def forward(zs, index, source=None):
        lower = zs < half
        to = jnp.where(lower, p - 1, p + 1)
        first = half_rows + zs * owned
        there = jnp.where(lower, first + rows, first - rows)
        ok = (z >= 1) & (to >= 0) & (to < n_prod)
        copy = pltpu.make_async_remote_copy(
            src_ref=slot(first) if source is None else source,
            dst_ref=slot(there),
            send_sem=halo_send.at[index],
            recv_sem=halo_recv.at[zs],
            device_id=(to, z),
            device_id_type=MESH,
        )

        @pl.when(ok)
        def _():
            copy.start()

        halos.append((ok, copy))

    forward(z, 0, pot_hbm)
    load_coup.start()
    load_rowb.start()
    order = [(target, j) for target in others + [z] for j in range(owned)]
    near_loads = []
    for step, (target, j) in enumerate(order):
        row = target * owned + j
        near_loads.append(
            pltpu.make_async_copy(near_hbm.at[row, 0], near.at[row], near_sem.at[step])
        )
        near_loads[-1].start()
    load_inj.start()
    load_inv.start()
    load_pot.wait()
    load_colb.wait()

    pot = band[pl.ds(own, owned)].reshape(owned * scen, panels)
    basis = colb[...].reshape(width, panels)
    products = lax.dot_general(
        pot,
        jnp.concatenate([basis] * (128 // width), axis=0),
        NT,
        preferred_element_type=jnp.float32,
    )
    lane = lax.broadcasted_iota(jnp.int32, (scen, 128), 1)
    inner = lane % width
    here = (lane // width) == p % (128 // width)
    mine_coef = jnp.zeros((scen, 128), jnp.float32)
    for j in range(owned):
        keep = here & (inner // rank_cap == j) & (inner % rank_cap < ranks_ref[j])
        mine_coef = jnp.where(keep, products[j * scen : (j + 1) * scen], mine_coef)
    coef[p] = mine_coef.astype(jnp.bfloat16)
    coef_copies = []
    for e in range(1, n_prod):
        coef_copies.append(
            pltpu.make_async_remote_copy(
                src_ref=coef.at[p],
                dst_ref=coef.at[p],
                send_sem=coef_send.at[e],
                recv_sem=coef_recv.at[p],
                device_id=((p + e) % n_prod, z),
                device_id_type=MESH,
            )
        )
        coef_copies[-1].start()

    def collect(index):
        zs = nearest[index]
        pltpu.make_async_remote_copy(
            src_ref=slot(half_rows + zs * owned),
            dst_ref=slot(half_rows + zs * owned),
            send_sem=gather_send.at[0],
            recv_sem=gather_recv.at[zs],
            device_id=(p, zs),
            device_id_type=MESH,
        ).wait_recv()
        forward(zs, index + 1)

    for index in range(n_pre - 1):
        collect(index)

    for e in range(1, n_prod):
        b = (p + e) % n_prod
        pltpu.make_async_remote_copy(
            src_ref=coef.at[b],
            dst_ref=coef.at[b],
            send_sem=coef_send.at[0],
            recv_sem=coef_recv.at[b],
            device_id=(b, z),
            device_id_type=MESH,
        ).wait_recv()
    load_coup.wait()
    load_rowb.wait()
    share = 128 // width
    blocks = []
    for m in range(n_prod // share):
        block = coef[m * share]
        for e in range(1, share):
            block = block + coef[m * share + e]
        blocks.append(block)
    columns = jnp.concatenate(blocks, axis=1)
    weights = lax.dot_general(
        columns,
        coup[...].reshape(rows * rank_cap, n_prod * width),
        NT,
        preferred_element_type=jnp.float32,
    )
    weights = jnp.concatenate([weights] * rows, axis=0)
    shape = (rows * scen, rows * rank_cap)
    row_of = lax.broadcasted_iota(jnp.int32, shape, 0) // scen
    col_of = lax.broadcasted_iota(jnp.int32, shape, 1) // rank_cap
    weights = jnp.where(row_of == col_of, weights, 0.0).astype(jnp.bfloat16)
    far[...] = jnp.dot(
        weights,
        rowb[...].reshape(rows * rank_cap, panels),
        preferred_element_type=jnp.float32,
    ).reshape(rows, scen, panels)

    for zs in range(n_pre):
        source = p + 1 if zs < half else p - 1
        first = half_rows + zs * owned + (rows if zs < half else -rows)

        @pl.when((z >= 1) & (source >= 0) & (source < n_prod))
        def _():
            pltpu.make_async_remote_copy(
                src_ref=slot(first),
                dst_ref=slot(first),
                send_sem=halo_send.at[0],
                recv_sem=halo_recv.at[zs],
                device_id=(source, z),
                device_id_type=MESH,
            ).wait_recv()

    offset = p * rows - half_rows

    def spread(value, j):
        blank = jnp.zeros((scen, panels), jnp.bfloat16)
        return jnp.concatenate([blank] * j + [value] + [blank] * (owned - 1 - j), axis=0)

    def apply(pairs):
        total = None
        for j, (block, value) in enumerate(pairs):
            term = lax.dot_general(
                block, spread(value, j), NT, preferred_element_type=jnp.float32
            )
            total = term if total is None else total + term
        return total.T

    def partial_rows(step, target):
        pairs = []
        for j in range(owned):
            near_loads[step * owned + j].wait()
            row = target * owned + j
            pairs.append((near[row], band[jnp.clip(cols_ref[row] - offset, 0, 2 * rows - 1)]))
        return apply(pairs).reshape(owned, scen, panels) + far[pl.ds(target * owned, owned)]

    parts = []
    for step, target in enumerate(others):
        sending[step] = partial_rows(step, target).astype(jnp.bfloat16)
        parts.append(
            pltpu.make_async_remote_copy(
                src_ref=sending.at[step],
                dst_ref=arriving.at[z],
                send_sem=part_send.at[step],
                recv_sem=part_recv.at[z],
                device_id=(p, target),
                device_id_type=MESH,
            )
        )
        parts[-1].start()
    load_inj.wait()
    mine[...] = inj[...] - partial_rows(n_pre - 1, z)
    load_inv.wait()
    residual = mine[...]
    for zs in nearest:
        pltpu.make_async_remote_copy(
            src_ref=arriving.at[zs],
            dst_ref=arriving.at[zs],
            send_sem=part_send.at[0],
            recv_sem=part_recv.at[zs],
            device_id=(p, zs),
            device_id_type=MESH,
        ).wait_recv()
        residual = residual - arriving[zs].astype(jnp.float32)
    res[...] = residual
    write_res = pltpu.make_async_copy(res, res_ref, out_sem.at[0])
    write_res.start()
    rounded = residual.astype(jnp.bfloat16)
    cor[...] = apply([(inv[j], rounded[j]) for j in range(owned)]).reshape(
        owned, scen, panels
    )
    write_cor = pltpu.make_async_copy(cor, cor_ref, out_sem.at[1])
    write_cor.start()
    write_res.wait()
    write_cor.wait()
    for copy in gathers + coef_copies + parts:
        copy.wait_send()
    for ok, copy in halos:

        @pl.when(ok)
        def _():
            copy.wait_send()


def hand_over(res_in, cor_in, res_out, cor_out, res, cor, sem):
    loads = [
        pltpu.make_async_copy(res_in, res, sem.at[0]),
        pltpu.make_async_copy(cor_in, cor, sem.at[1]),
    ]
    stores = [
        pltpu.make_async_copy(res, res_out, sem.at[2]),
        pltpu.make_async_copy(cor, cor_out, sem.at[3]),
    ]
    for copy in loads:
        copy.start()
    for load, store in zip(loads, stores):
        load.wait()
        store.start()
    for copy in stores:
        copy.wait()


def local(n_prod, n_pre, potentials, injected, near, cols, rowb, colb, ranks, coup, inv):
    owned, scen, panels = potentials.shape
    rows = near.shape[0]
    out = jax.ShapeDtypeStruct(injected.shape, jnp.float32)
    anywhere = pl.BlockSpec(memory_space=pltpu.HBM)
    scalars = pl.BlockSpec(memory_space=pltpu.SMEM)
    dma = pltpu.SemaphoreType.DMA
    blocks = rows + owned
    residual, corrected = pl.pallas_call(
        functools.partial(kernel, n_prod, n_pre),
        out_shape=(out, out),
        in_specs=[
            anywhere,
            anywhere,
            anywhere,
            scalars,
            anywhere,
            anywhere,
            scalars,
            anywhere,
            anywhere,
        ],
        out_specs=(anywhere, anywhere),
        scratch_shapes=[
            pltpu.VMEM((2 * rows, scen, panels), jnp.bfloat16),
            pltpu.VMEM(injected.shape, jnp.float32),
            pltpu.VMEM((rows, panels, panels), jnp.bfloat16),
            pltpu.VMEM(rowb.shape, jnp.bfloat16),
            pltpu.VMEM(colb.shape, jnp.bfloat16),
            pltpu.VMEM(coup.shape, jnp.bfloat16),
            pltpu.VMEM(inv.shape, jnp.bfloat16),
            pltpu.VMEM((n_prod, scen, 128), jnp.bfloat16),
            pltpu.VMEM((rows, scen, panels), jnp.float32),
            pltpu.VMEM(injected.shape, jnp.float32),
            pltpu.VMEM(injected.shape, jnp.float32),
            pltpu.VMEM(injected.shape, jnp.float32),
            pltpu.VMEM((n_pre - 1, owned, scen, panels), jnp.bfloat16),
            pltpu.VMEM((n_pre, owned, scen, panels), jnp.bfloat16),
            dma((6,)),
            dma((rows,)),
            dma((n_pre,)),
            dma((n_pre,)),
            dma((n_pre,)),
            dma((n_pre,)),
            dma((n_prod,)),
            dma((n_prod,)),
            dma((n_pre,)),
            dma((n_pre,)),
            dma((2,)),
        ],
        compiler_params=pltpu.CompilerParams(
            collective_id=0, has_side_effects=True, vmem_limit_bytes=63 * 2**20
        ),
        cost_estimate=pl.CostEstimate(
            flops=2 * blocks * scen * panels * panels,
            bytes_accessed=2 * blocks * panels * panels,
            transcendentals=0,
        ),
    )(potentials, injected, near, cols.reshape(rows), rowb, colb, ranks, coup, inv)
    return pl.pallas_call(
        hand_over,
        out_shape=(out, out),
        in_specs=[anywhere, anywhere],
        out_specs=(anywhere, anywhere),
        scratch_shapes=[
            pltpu.VMEM(injected.shape, jnp.float32),
            pltpu.VMEM(injected.shape, jnp.float32),
            dma((4,)),
        ],
        compiler_params=pltpu.CompilerParams(vmem_limit_bytes=63 * 2**20),
    )(residual, corrected)


def solution(mesh):
    return jax.shard_map(
        functools.partial(local, mesh.shape["prod"], mesh.shape["pre"]),
        mesh=mesh,
        in_specs=(
            P(("prod", "pre"), None, None),
            P(("prod", "pre"), None, None),
            P("prod", "pre", None, None),
            P("prod", "pre"),
            P("prod", None, None),
            P(("prod", "pre"), None, None),
            P(("prod", "pre")),
            P("prod", None, "pre"),
            P(("prod", "pre"), None, None),
        ),
        out_specs=(P(("prod", "pre"), None, None), P(("prod", "pre"), None, None)),
        check_vma=False,
    )
```

```python
import functools

import jax
import jax.numpy as jnp
from jax import lax
from jax.experimental import pallas as pl
from jax.experimental.pallas import tpu as pltpu
from jax.sharding import PartitionSpec as P

MESH = pl.DeviceIdType.MESH
NT = (((1,), (1,)), ((), ()))


def kernel(
    n_prod,
    n_pre,
    pot_hbm,
    inj_hbm,
    near_hbm,
    cols_ref,
    rowb_hbm,
    colb_hbm,
    ranks_ref,
    coup_hbm,
    inv_hbm,
    res_ref,
    cor_ref,
    group,
    soon,
    late,
    inj,
    near,
    rowb,
    colb,
    coup,
    inv,
    coef,
    far,
    mine,
    res,
    cor,
    sending,
    arriving,
    load_sem,
    near_sem,
    gather_send,
    gather_recv,
    halo_send,
    halo_recv,
    coef_send,
    coef_recv,
    part_send,
    part_recv,
    out_sem,
):
    owned, scen, panels = pot_hbm.shape
    rows = near_hbm.shape[0]
    rank_cap = colb_hbm.shape[1]
    half_rows = rows // 2
    half = n_pre // 2
    width = owned * rank_cap
    p = lax.axis_index("prod")
    z = lax.axis_index("pre")
    high, low = z // half, z % half
    others = [(1 - high) * half + (low + e) % half for e in range(half)]
    others += [high * half + (low + e) % half for e in range(1, half)]
    nearest = others[half:] + others[:half]

    def slot(first):
        return group.at[pl.ds(first * owned, owned)]

    load_pot = pltpu.make_async_copy(pot_hbm, slot(z), load_sem.at[0])
    load_colb = pltpu.make_async_copy(colb_hbm, colb, load_sem.at[1])
    load_coup = pltpu.make_async_copy(coup_hbm, coup, load_sem.at[2])
    load_rowb = pltpu.make_async_copy(rowb_hbm, rowb, load_sem.at[3])
    load_inj = pltpu.make_async_copy(inj_hbm, inj, load_sem.at[4])
    load_inv = pltpu.make_async_copy(inv_hbm, inv, load_sem.at[5])
    load_pot.start()
    load_colb.start()

    barrier = pltpu.get_barrier_semaphore()
    for target in others:
        pl.semaphore_signal(barrier, inc=1, device_id=(p, target), device_id_type=MESH)
    for e in range(1, n_prod):
        pl.semaphore_signal(
            barrier, inc=1, device_id=((p + e) % n_prod, z), device_id_type=MESH
        )
    pl.semaphore_wait(barrier, n_pre - 1 + n_prod - 1)

    gathers = []
    for e, target in enumerate(others):
        gathers.append(
            pltpu.make_async_remote_copy(
                src_ref=pot_hbm,
                dst_ref=slot(z),
                send_sem=gather_send.at[e],
                recv_sem=gather_recv.at[z],
                device_id=(p, target),
                device_id_type=MESH,
            )
        )
        gathers[-1].start()

    halos = []
    odd = p % 2
    mate, side = p + 1 - 2 * odd, 1 - odd

    def halo_copy(buffer, zs, send, source, to):
        return pltpu.make_async_remote_copy(
            src_ref=source,
            dst_ref=buffer.at[pl.ds(zs % half * owned, owned)],
            send_sem=halo_send.at[send],
            recv_sem=halo_recv.at[zs],
            device_id=(to, z),
            device_id_type=MESH,
        )

    def forward(zs, index, source=None):
        source = slot(zs) if source is None else source
        to = jnp.where(zs < half, p - 1, p + 1)
        near_by = (z >= 1) & (to == mate)
        far_off = (z >= 1) & (to != mate) & (to >= 0) & (to < n_prod)
        for ok, buffer in ((near_by, soon), (far_off, late)):
            copy = halo_copy(buffer, zs, index, source, to)

            @pl.when(ok)
            def _():
                copy.start()

            halos.append((ok, copy))

    def await_halo(buffer, upper, from_device):
        @pl.when((z >= 1) & (from_device >= 0) & (from_device < n_prod))
        def _():
            for e in range(half):
                zs = (1 - upper) * half + e
                halo_copy(buffer, zs, 0, slot(zs), from_device).wait_recv()

    forward(z, 0, pot_hbm)
    load_coup.start()
    load_rowb.start()
    same = side == high
    cross, beside = others[:half], others[half:]
    orders = (cross + beside + [z], beside + cross + [z])

    def near_load(row):
        return pltpu.make_async_copy(near_hbm.at[row, 0], near.at[row], near_sem.at[row])

    for first, second in zip(*orders):
        for j in range(owned):
            near_load(jnp.where(same, second, first) * owned + j).start()
    load_inj.start()
    load_inv.start()
    load_pot.wait()
    load_colb.wait()

    pot = group[pl.ds(z * owned, owned)].reshape(owned * scen, panels)
    basis = colb[...].reshape(width, panels)
    products = lax.dot_general(
        pot,
        jnp.concatenate([basis] * (128 // width), axis=0),
        NT,
        preferred_element_type=jnp.float32,
    )
    lane = lax.broadcasted_iota(jnp.int32, (scen, 128), 1)
    inner = lane % width
    here = (lane // width) == p % (128 // width)
    mine_coef = jnp.zeros((scen, 128), jnp.float32)
    for j in range(owned):
        keep = here & (inner // rank_cap == j) & (inner % rank_cap < ranks_ref[j])
        mine_coef = jnp.where(keep, products[j * scen : (j + 1) * scen], mine_coef)
    coef[p] = mine_coef.astype(jnp.bfloat16)
    coef_copies = []
    for e in range(1, n_prod):
        coef_copies.append(
            pltpu.make_async_remote_copy(
                src_ref=coef.at[p],
                dst_ref=coef.at[p],
                send_sem=coef_send.at[e],
                recv_sem=coef_recv.at[p],
                device_id=((p + e) % n_prod, z),
                device_id_type=MESH,
            )
        )
        coef_copies[-1].start()

    def collect(index):
        zs = nearest[index]
        pltpu.make_async_remote_copy(
            src_ref=slot(zs),
            dst_ref=slot(zs),
            send_sem=gather_send.at[0],
            recv_sem=gather_recv.at[zs],
            device_id=(p, zs),
            device_id_type=MESH,
        ).wait_recv()
        forward(zs, index + 1)

    for index in range(n_pre - 1):
        collect(index)

    for e in range(1, n_prod):
        b = (p + e) % n_prod
        pltpu.make_async_remote_copy(
            src_ref=coef.at[b],
            dst_ref=coef.at[b],
            send_sem=coef_send.at[0],
            recv_sem=coef_recv.at[b],
            device_id=(b, z),
            device_id_type=MESH,
        ).wait_recv()
    load_coup.wait()
    load_rowb.wait()
    share = 128 // width
    blocks = []
    for m in range(n_prod // share):
        block = coef[m * share]
        for e in range(1, share):
            block = block + coef[m * share + e]
        blocks.append(block)
    columns = jnp.concatenate(blocks, axis=1)
    weights = lax.dot_general(
        columns,
        coup[...].reshape(rows * rank_cap, n_prod * width),
        NT,
        preferred_element_type=jnp.float32,
    )
    weights = jnp.concatenate([weights] * rows, axis=0)
    shape = (rows * scen, rows * rank_cap)
    row_of = lax.broadcasted_iota(jnp.int32, shape, 0) // scen
    col_of = lax.broadcasted_iota(jnp.int32, shape, 1) // rank_cap
    weights = jnp.where(row_of == col_of, weights, 0.0).astype(jnp.bfloat16)
    far[...] = jnp.dot(
        weights,
        rowb[...].reshape(rows * rank_cap, panels),
        preferred_element_type=jnp.float32,
    ).reshape(rows, scen, panels)

    offset = p * rows

    def partial_row(row, buffer, upper):
        index = cols_ref[row] - offset
        beyond = jnp.where(upper == 1, index - rows, index + half_rows)
        outside = (index < 0) | (index >= rows)
        picked = jnp.where(
            outside,
            buffer[jnp.clip(beyond, 0, half_rows - 1)],
            group[jnp.clip(index, 0, rows - 1)],
        )
        near_load(row).wait()
        value = lax.dot_general(picked, near[row], NT, preferred_element_type=jnp.float32)
        return value + far[row]

    def part_copy(target, j):
        return pltpu.make_async_remote_copy(
            src_ref=sending.at[target, j],
            dst_ref=arriving.at[z, j],
            send_sem=part_send.at[target, j],
            recv_sem=part_recv.at[z, j],
            device_id=(p, target),
            device_id_type=MESH,
        )

    def send_rows(targets, buffer, upper):
        for target in targets:
            for j in range(owned):
                value = partial_row(target * owned + j, buffer, upper)
                sending[target, j] = value.astype(jnp.bfloat16)
                part_copy(target, j).start()

    def keep_rows(buffer, upper):
        for j in range(owned):
            mine[j] = inj[j] - partial_row(z * owned + j, buffer, upper)

    other = p - 1 + 2 * odd
    await_halo(soon, side, mate)
    load_inj.wait()

    @pl.when(same)
    def _():
        send_rows(beside, soon, side)
        await_halo(late, 1 - side, other)
        send_rows(cross, late, 1 - side)
        keep_rows(soon, side)

    @pl.when(jnp.logical_not(same))
    def _():
        send_rows(cross, soon, side)
        await_halo(late, 1 - side, other)
        send_rows(beside, late, 1 - side)
        keep_rows(late, 1 - side)

    load_inv.wait()
    writes = []
    for j in range(owned):
        residual = mine[j]
        for zs in nearest:
            pltpu.make_async_remote_copy(
                src_ref=arriving.at[zs, j],
                dst_ref=arriving.at[zs, j],
                send_sem=part_send.at[zs, j],
                recv_sem=part_recv.at[zs, j],
                device_id=(p, zs),
                device_id_type=MESH,
            ).wait_recv()
            residual = residual - arriving[zs, j].astype(jnp.float32)
        res[j] = residual
        writes.append(pltpu.make_async_copy(res.at[j], res_ref.at[j], out_sem.at[0, j]))
        writes[-1].start()
        cor[j] = lax.dot_general(
            residual.astype(jnp.bfloat16), inv[j], NT, preferred_element_type=jnp.float32
        )
        writes.append(pltpu.make_async_copy(cor.at[j], cor_ref.at[j], out_sem.at[1, j]))
        writes[-1].start()
    for copy in writes:
        copy.wait()
    parts = [part_copy(target, j) for target in others for j in range(owned)]
    for copy in gathers + coef_copies + parts:
        copy.wait_send()
    for ok, copy in halos:

        @pl.when(ok)
        def _():
            copy.wait_send()


def hand_over(res_in, cor_in, res_out, cor_out, res, cor, sem):
    loads = [
        pltpu.make_async_copy(res_in, res, sem.at[0]),
        pltpu.make_async_copy(cor_in, cor, sem.at[1]),
    ]
    stores = [
        pltpu.make_async_copy(res, res_out, sem.at[2]),
        pltpu.make_async_copy(cor, cor_out, sem.at[3]),
    ]
    for copy in loads:
        copy.start()
    for load, store in zip(loads, stores):
        load.wait()
        store.start()
    for copy in stores:
        copy.wait()


def local(n_prod, n_pre, potentials, injected, near, cols, rowb, colb, ranks, coup, inv):
    owned, scen, panels = potentials.shape
    rows = near.shape[0]
    out = jax.ShapeDtypeStruct(injected.shape, jnp.float32)
    anywhere = pl.BlockSpec(memory_space=pltpu.HBM)
    scalars = pl.BlockSpec(memory_space=pltpu.SMEM)
    dma = pltpu.SemaphoreType.DMA
    blocks = rows + owned
    residual, corrected = pl.pallas_call(
        functools.partial(kernel, n_prod, n_pre),
        out_shape=(out, out),
        in_specs=[
            anywhere,
            anywhere,
            anywhere,
            scalars,
            anywhere,
            anywhere,
            scalars,
            anywhere,
            anywhere,
        ],
        out_specs=(anywhere, anywhere),
        scratch_shapes=[
            pltpu.VMEM((rows, scen, panels), jnp.bfloat16),
            pltpu.VMEM((rows // 2, scen, panels), jnp.bfloat16),
            pltpu.VMEM((rows // 2, scen, panels), jnp.bfloat16),
            pltpu.VMEM(injected.shape, jnp.float32),
            pltpu.VMEM((rows, panels, panels), jnp.bfloat16),
            pltpu.VMEM(rowb.shape, jnp.bfloat16),
            pltpu.VMEM(colb.shape, jnp.bfloat16),
            pltpu.VMEM(coup.shape, jnp.bfloat16),
            pltpu.VMEM(inv.shape, jnp.bfloat16),
            pltpu.VMEM((n_prod, scen, 128), jnp.bfloat16),
            pltpu.VMEM((rows, scen, panels), jnp.float32),
            pltpu.VMEM(injected.shape, jnp.float32),
            pltpu.VMEM(injected.shape, jnp.float32),
            pltpu.VMEM(injected.shape, jnp.float32),
            pltpu.VMEM((n_pre, owned, scen, panels), jnp.bfloat16),
            pltpu.VMEM((n_pre, owned, scen, panels), jnp.bfloat16),
            dma((6,)),
            dma((rows,)),
            dma((n_pre,)),
            dma((n_pre,)),
            dma((n_pre,)),
            dma((n_pre,)),
            dma((n_prod,)),
            dma((n_prod,)),
            dma((n_pre, owned)),
            dma((n_pre, owned)),
            dma((2, owned)),
        ],
        compiler_params=pltpu.CompilerParams(
            collective_id=0, has_side_effects=True, vmem_limit_bytes=63 * 2**20
        ),
        cost_estimate=pl.CostEstimate(
            flops=2 * blocks * scen * panels * panels,
            bytes_accessed=2 * blocks * panels * panels,
            transcendentals=0,
        ),
    )(potentials, injected, near, cols.reshape(rows), rowb, colb, ranks, coup, inv)
    return pl.pallas_call(
        hand_over,
        out_shape=(out, out),
        in_specs=[anywhere, anywhere],
        out_specs=(anywhere, anywhere),
        scratch_shapes=[
            pltpu.VMEM(injected.shape, jnp.float32),
            pltpu.VMEM(injected.shape, jnp.float32),
            dma((4,)),
        ],
        compiler_params=pltpu.CompilerParams(vmem_limit_bytes=63 * 2**20),
    )(residual, corrected)


def solution(mesh):
    return jax.shard_map(
        functools.partial(local, mesh.shape["prod"], mesh.shape["pre"]),
        mesh=mesh,
        in_specs=(
            P(("prod", "pre"), None, None),
            P(("prod", "pre"), None, None),
            P("prod", "pre", None, None),
            P("prod", "pre"),
            P("prod", None, None),
            P(("prod", "pre"), None, None),
            P(("prod", "pre")),
            P("prod", None, "pre"),
            P(("prod", "pre"), None, None),
        ),
        out_specs=(P(("prod", "pre"), None, None), P(("prod", "pre"), None, None)),
        check_vma=False,
    )
```

```python
import functools

import jax
import jax.numpy as jnp
from jax import lax
from jax.experimental import pallas as pl
from jax.experimental.pallas import tpu as pltpu
from jax.sharding import PartitionSpec as P

MESH = pl.DeviceIdType.MESH
NT = (((1,), (1,)), ((), ()))


def kernel(
    n_prod,
    n_pre,
    pot_hbm,
    inj_hbm,
    near_hbm,
    cols_ref,
    rowb_hbm,
    colb_hbm,
    ranks_ref,
    coup_hbm,
    inv_hbm,
    res_ref,
    cor_ref,
    group,
    soon,
    late,
    inj,
    near,
    rowb,
    colb,
    coup,
    inv,
    coef,
    far,
    mine,
    res,
    cor,
    sending,
    arriving,
    load_sem,
    near_sem,
    gather_send,
    gather_recv,
    halo_send,
    halo_recv,
    coef_send,
    coef_recv,
    part_send,
    part_recv,
    out_sem,
):
    owned, scen, panels = pot_hbm.shape
    rows = near_hbm.shape[0]
    rank_cap = colb_hbm.shape[1]
    half_rows = rows // 2
    half = n_pre // 2
    width = owned * rank_cap
    p = lax.axis_index("prod")
    z = lax.axis_index("pre")
    high, low = z // half, z % half
    others = [(1 - high) * half + (low + e) % half for e in range(half)]
    others += [high * half + (low + e) % half for e in range(1, half)]
    nearest = others[half:] + others[:half]

    def slot(first):
        return group.at[pl.ds(first * owned, owned)]

    load_pot = pltpu.make_async_copy(pot_hbm, slot(z), load_sem.at[0])
    load_colb = pltpu.make_async_copy(colb_hbm, colb, load_sem.at[1])
    load_coup = pltpu.make_async_copy(coup_hbm, coup, load_sem.at[2])
    load_rowb = pltpu.make_async_copy(rowb_hbm, rowb, load_sem.at[3])
    load_inj = pltpu.make_async_copy(inj_hbm, inj, load_sem.at[4])
    load_inv = pltpu.make_async_copy(inv_hbm, inv, load_sem.at[5])
    load_pot.start()
    load_colb.start()

    barrier = pltpu.get_barrier_semaphore()
    for target in others:
        pl.semaphore_signal(barrier, inc=1, device_id=(p, target), device_id_type=MESH)
    for e in range(1, n_prod):
        pl.semaphore_signal(
            barrier, inc=1, device_id=((p + e) % n_prod, z), device_id_type=MESH
        )
    pl.semaphore_wait(barrier, n_pre - 1 + n_prod - 1)

    gathers = []
    for e, target in enumerate(others):
        gathers.append(
            pltpu.make_async_remote_copy(
                src_ref=pot_hbm,
                dst_ref=slot(z),
                send_sem=gather_send.at[e],
                recv_sem=gather_recv.at[z],
                device_id=(p, target),
                device_id_type=MESH,
            )
        )
        gathers[-1].start()

    halos = []
    odd = p % 2
    mate, side = p + 1 - 2 * odd, 1 - odd

    def halo_copy(buffer, zs, send, source, to):
        return pltpu.make_async_remote_copy(
            src_ref=source,
            dst_ref=buffer.at[pl.ds(zs % half * owned, owned)],
            send_sem=halo_send.at[send],
            recv_sem=halo_recv.at[zs],
            device_id=(to, z),
            device_id_type=MESH,
        )

    def forward(zs, index, source=None):
        source = slot(zs) if source is None else source
        to = jnp.where(zs < half, p - 1, p + 1)
        near_by = (z >= 1) & (to == mate)
        far_off = (z >= 1) & (to != mate) & (to >= 0) & (to < n_prod)
        for ok, buffer in ((near_by, soon), (far_off, late)):
            copy = halo_copy(buffer, zs, index, source, to)

            @pl.when(ok)
            def _():
                copy.start()

            halos.append((ok, copy))

    def await_halo(buffer, upper, from_device):
        @pl.when((z >= 1) & (from_device >= 0) & (from_device < n_prod))
        def _():
            for e in range(half):
                zs = (1 - upper) * half + e
                halo_copy(buffer, zs, 0, slot(zs), from_device).wait_recv()

    forward(z, 0, pot_hbm)
    load_coup.start()
    load_rowb.start()
    same = (side == high) & (z >= 1)
    cross, beside = others[:half], others[half:]
    orders = (cross + beside + [z], beside + cross + [z])

    def near_load(row):
        return pltpu.make_async_copy(near_hbm.at[row, 0], near.at[row], near_sem.at[row])

    for first, second in zip(*orders):
        for j in range(owned):
            near_load(jnp.where(same, second, first) * owned + j).start()
    load_inj.start()
    load_inv.start()
    load_pot.wait()
    load_colb.wait()

    pot = group[pl.ds(z * owned, owned)].reshape(owned * scen, panels)
    basis = colb[...].reshape(width, panels)
    products = lax.dot_general(
        pot,
        jnp.concatenate([basis] * (128 // width), axis=0),
        NT,
        preferred_element_type=jnp.float32,
    )
    lane = lax.broadcasted_iota(jnp.int32, (scen, 128), 1)
    inner = lane % width
    here = (lane // width) == p % (128 // width)
    mine_coef = jnp.zeros((scen, 128), jnp.float32)
    for j in range(owned):
        keep = here & (inner // rank_cap == j) & (inner % rank_cap < ranks_ref[j])
        mine_coef = jnp.where(keep, products[j * scen : (j + 1) * scen], mine_coef)
    coef[p] = mine_coef.astype(jnp.bfloat16)
    coef_copies = []
    for e in range(1, n_prod):
        coef_copies.append(
            pltpu.make_async_remote_copy(
                src_ref=coef.at[p],
                dst_ref=coef.at[p],
                send_sem=coef_send.at[e],
                recv_sem=coef_recv.at[p],
                device_id=((p + e) % n_prod, z),
                device_id_type=MESH,
            )
        )
        coef_copies[-1].start()

    def collect(index):
        zs = nearest[index]
        pltpu.make_async_remote_copy(
            src_ref=slot(zs),
            dst_ref=slot(zs),
            send_sem=gather_send.at[0],
            recv_sem=gather_recv.at[zs],
            device_id=(p, zs),
            device_id_type=MESH,
        ).wait_recv()
        forward(zs, index + 1)

    for index in range(n_pre - 1):
        collect(index)

    for e in range(1, n_prod):
        b = (p + e) % n_prod
        pltpu.make_async_remote_copy(
            src_ref=coef.at[b],
            dst_ref=coef.at[b],
            send_sem=coef_send.at[0],
            recv_sem=coef_recv.at[b],
            device_id=(b, z),
            device_id_type=MESH,
        ).wait_recv()
    load_coup.wait()
    load_rowb.wait()
    share = 128 // width
    blocks = []
    for m in range(n_prod // share):
        block = coef[m * share]
        for e in range(1, share):
            block = block + coef[m * share + e]
        blocks.append(block)
    columns = jnp.concatenate(blocks, axis=1)
    weights = lax.dot_general(
        columns,
        coup[...].reshape(rows * rank_cap, n_prod * width),
        NT,
        preferred_element_type=jnp.float32,
    )
    weights = jnp.concatenate([weights] * rows, axis=0)
    shape = (rows * scen, rows * rank_cap)
    row_of = lax.broadcasted_iota(jnp.int32, shape, 0) // scen
    col_of = lax.broadcasted_iota(jnp.int32, shape, 1) // rank_cap
    weights = jnp.where(row_of == col_of, weights, 0.0).astype(jnp.bfloat16)
    far[...] = jnp.dot(
        weights,
        rowb[...].reshape(rows * rank_cap, panels),
        preferred_element_type=jnp.float32,
    ).reshape(rows, scen, panels)

    offset = p * rows

    def partial_row(row, buffer, upper):
        index = cols_ref[row] - offset
        beyond = jnp.where(upper == 1, index - rows, index + half_rows)
        outside = (index < 0) | (index >= rows)
        picked = jnp.where(
            outside,
            buffer[jnp.clip(beyond, 0, half_rows - 1)],
            group[jnp.clip(index, 0, rows - 1)],
        )
        value = lax.dot_general(picked, near[row], NT, preferred_element_type=jnp.float32)
        return value + far[row]

    def part_copy(target):
        return pltpu.make_async_remote_copy(
            src_ref=sending.at[target],
            dst_ref=arriving.at[z],
            send_sem=part_send.at[target],
            recv_sem=part_recv.at[z],
            device_id=(p, target),
            device_id_type=MESH,
        )

    def rows_of(target, buffer, upper):
        return [partial_row(target * owned + j, buffer, upper) for j in range(owned)]

    def send_rows(targets, buffer, upper):
        for target in targets:
            for j, value in enumerate(rows_of(target, buffer, upper)):
                sending[target, j] = value.astype(jnp.bfloat16)
            part_copy(target).start()

    def keep_rows(buffer, upper):
        for j, value in enumerate(rows_of(z, buffer, upper)):
            mine[j] = inj[j] - value

    other = p - 1 + 2 * odd
    for row in range(rows):
        near_load(row).wait()
    load_inj.wait()
    load_inv.wait()
    await_halo(soon, side, mate)

    @pl.when(same)
    def _():
        send_rows(beside, soon, side)
        await_halo(late, 1 - side, other)
        send_rows(cross, late, 1 - side)
        keep_rows(soon, side)

    @pl.when(jnp.logical_not(same))
    def _():
        send_rows(cross, soon, side)
        await_halo(late, 1 - side, other)
        send_rows(beside, late, 1 - side)
        keep_rows(late, 1 - side)

    for zs in nearest:
        pltpu.make_async_remote_copy(
            src_ref=arriving.at[zs],
            dst_ref=arriving.at[zs],
            send_sem=part_send.at[zs],
            recv_sem=part_recv.at[zs],
            device_id=(p, zs),
            device_id_type=MESH,
        ).wait_recv()
    residual = mine[...]
    for zs in nearest:
        residual = residual - arriving[zs].astype(jnp.float32)
    res[...] = residual
    write_res = pltpu.make_async_copy(res, res_ref, out_sem.at[0])
    write_res.start()
    rounded = residual.astype(jnp.bfloat16)
    for j in range(owned):
        cor[j] = lax.dot_general(
            rounded[j], inv[j], NT, preferred_element_type=jnp.float32
        )
    write_cor = pltpu.make_async_copy(cor, cor_ref, out_sem.at[1])
    write_cor.start()
    write_res.wait()
    write_cor.wait()
    parts = [part_copy(target) for target in others]
    for copy in gathers + coef_copies + parts:
        copy.wait_send()
    for ok, copy in halos:

        @pl.when(ok)
        def _():
            copy.wait_send()


def hand_over(res_in, cor_in, res_out, cor_out, res, cor, sem):
    loads = [
        pltpu.make_async_copy(res_in, res, sem.at[0]),
        pltpu.make_async_copy(cor_in, cor, sem.at[1]),
    ]
    stores = [
        pltpu.make_async_copy(res, res_out, sem.at[2]),
        pltpu.make_async_copy(cor, cor_out, sem.at[3]),
    ]
    for copy in loads:
        copy.start()
    for load, store in zip(loads, stores):
        load.wait()
        store.start()
    for copy in stores:
        copy.wait()


def local(n_prod, n_pre, potentials, injected, near, cols, rowb, colb, ranks, coup, inv):
    owned, scen, panels = potentials.shape
    rows = near.shape[0]
    out = jax.ShapeDtypeStruct(injected.shape, jnp.float32)
    anywhere = pl.BlockSpec(memory_space=pltpu.HBM)
    scalars = pl.BlockSpec(memory_space=pltpu.SMEM)
    dma = pltpu.SemaphoreType.DMA
    blocks = rows + owned
    residual, corrected = pl.pallas_call(
        functools.partial(kernel, n_prod, n_pre),
        out_shape=(out, out),
        in_specs=[
            anywhere,
            anywhere,
            anywhere,
            scalars,
            anywhere,
            anywhere,
            scalars,
            anywhere,
            anywhere,
        ],
        out_specs=(anywhere, anywhere),
        scratch_shapes=[
            pltpu.VMEM((rows, scen, panels), jnp.bfloat16),
            pltpu.VMEM((rows // 2, scen, panels), jnp.bfloat16),
            pltpu.VMEM((rows // 2, scen, panels), jnp.bfloat16),
            pltpu.VMEM(injected.shape, jnp.float32),
            pltpu.VMEM((rows, panels, panels), jnp.bfloat16),
            pltpu.VMEM(rowb.shape, jnp.bfloat16),
            pltpu.VMEM(colb.shape, jnp.bfloat16),
            pltpu.VMEM(coup.shape, jnp.bfloat16),
            pltpu.VMEM(inv.shape, jnp.bfloat16),
            pltpu.VMEM((n_prod, scen, 128), jnp.bfloat16),
            pltpu.VMEM((rows, scen, panels), jnp.float32),
            pltpu.VMEM(injected.shape, jnp.float32),
            pltpu.VMEM(injected.shape, jnp.float32),
            pltpu.VMEM(injected.shape, jnp.float32),
            pltpu.VMEM((n_pre, owned, scen, panels), jnp.bfloat16),
            pltpu.VMEM((n_pre, owned, scen, panels), jnp.bfloat16),
            dma((6,)),
            dma((rows,)),
            dma((n_pre,)),
            dma((n_pre,)),
            dma((n_pre,)),
            dma((n_pre,)),
            dma((n_prod,)),
            dma((n_prod,)),
            dma((n_pre,)),
            dma((n_pre,)),
            dma((2,)),
        ],
        compiler_params=pltpu.CompilerParams(
            collective_id=0, has_side_effects=True, vmem_limit_bytes=63 * 2**20
        ),
        cost_estimate=pl.CostEstimate(
            flops=2 * blocks * scen * panels * panels,
            bytes_accessed=2 * blocks * panels * panels,
            transcendentals=0,
        ),
    )(potentials, injected, near, cols.reshape(rows), rowb, colb, ranks, coup, inv)
    return pl.pallas_call(
        hand_over,
        out_shape=(out, out),
        in_specs=[anywhere, anywhere],
        out_specs=(anywhere, anywhere),
        scratch_shapes=[
            pltpu.VMEM(injected.shape, jnp.float32),
            pltpu.VMEM(injected.shape, jnp.float32),
            dma((4,)),
        ],
        compiler_params=pltpu.CompilerParams(vmem_limit_bytes=63 * 2**20),
    )(residual, corrected)


def solution(mesh):
    return jax.shard_map(
        functools.partial(local, mesh.shape["prod"], mesh.shape["pre"]),
        mesh=mesh,
        in_specs=(
            P(("prod", "pre"), None, None),
            P(("prod", "pre"), None, None),
            P("prod", "pre", None, None),
            P("prod", "pre"),
            P("prod", None, None),
            P(("prod", "pre"), None, None),
            P(("prod", "pre")),
            P("prod", None, "pre"),
            P(("prod", "pre"), None, None),
        ),
        out_specs=(P(("prod", "pre"), None, None), P(("prod", "pre"), None, None)),
        check_vma=False,
    )
```

```python
import functools

import jax
import jax.numpy as jnp
from jax import lax
from jax.experimental import pallas as pl
from jax.experimental.pallas import tpu as pltpu
from jax.sharding import PartitionSpec as P

MESH = pl.DeviceIdType.MESH
NT = (((1,), (1,)), ((), ()))


def kernel(
    n_prod,
    n_pre,
    pot_hbm,
    inj_hbm,
    near_hbm,
    cols_ref,
    rowb_hbm,
    colb_hbm,
    ranks_ref,
    coup_hbm,
    inv_hbm,
    res_ref,
    cor_ref,
    group,
    early,
    later,
    inj,
    near,
    rowb,
    colb,
    coup,
    inv,
    coef,
    far,
    mine,
    sending,
    arriving,
    load_sem,
    near_sem,
    gather_send,
    gather_recv,
    halo_send,
    halo_recv,
    coef_send,
    coef_recv,
    part_send,
    part_recv,
):
    owned, scen, panels = pot_hbm.shape
    rows = near_hbm.shape[0]
    rank_cap = colb_hbm.shape[1]
    half_rows = rows // 2
    half = n_pre // 2
    width = owned * rank_cap
    p = lax.axis_index("prod")
    z = lax.axis_index("pre")
    high, low = z // half, z % half
    others = [(1 - high) * half + (low + e) % half for e in range(half)]
    others += [high * half + (low + e) % half for e in range(1, half)]
    nearest = others[half:] + others[:half]

    def slot(first):
        return group.at[pl.ds(first * owned, owned)]

    load_pot = pltpu.make_async_copy(pot_hbm, slot(z), load_sem.at[0])
    load_colb = pltpu.make_async_copy(colb_hbm, colb, load_sem.at[1])
    load_coup = pltpu.make_async_copy(coup_hbm, coup, load_sem.at[2])
    load_rowb = pltpu.make_async_copy(rowb_hbm, rowb, load_sem.at[3])
    load_inj = pltpu.make_async_copy(inj_hbm, inj, load_sem.at[4])
    load_inv = pltpu.make_async_copy(inv_hbm, inv, load_sem.at[5])
    load_pot.start()
    load_colb.start()

    barrier = pltpu.get_barrier_semaphore()
    for target in others:
        pl.semaphore_signal(barrier, inc=1, device_id=(p, target), device_id_type=MESH)
    for e in range(1, n_prod):
        pl.semaphore_signal(
            barrier, inc=1, device_id=((p + e) % n_prod, z), device_id_type=MESH
        )
    pl.semaphore_wait(barrier, n_pre - 1 + n_prod - 1)

    gathers = []
    for e, target in enumerate(others):
        gathers.append(
            pltpu.make_async_remote_copy(
                src_ref=pot_hbm,
                dst_ref=slot(z),
                send_sem=gather_send.at[e],
                recv_sem=gather_recv.at[z],
                device_id=(p, target),
                device_id_type=MESH,
            )
        )
        gathers[-1].start()

    halos = []

    def halo_copy(buffer, zs, send, source, to):
        return pltpu.make_async_remote_copy(
            src_ref=source,
            dst_ref=buffer.at[pl.ds(zs % half * owned, owned)],
            send_sem=halo_send.at[send],
            recv_sem=halo_recv.at[zs],
            device_id=(to, z),
            device_id_type=MESH,
        )

    def forward(zs, index, buffer, source=None):
        source = slot(zs) if source is None else source
        to = jnp.where(zs < half, p - 1, p + 1)
        ok = (z >= 1) & (to >= 0) & (to < n_prod)
        copy = halo_copy(buffer, zs, index, source, to)

        @pl.when(ok)
        def _():
            copy.start()

        halos.append((ok, copy))

    def await_halo(buffer, upper):
        source = p - 1 + 2 * upper

        @pl.when((z >= 1) & (source >= 0) & (source < n_prod))
        def _():
            for e in range(half):
                zs = (1 - upper) * half + e
                halo_copy(buffer, zs, 0, slot(zs), source).wait_recv()

    forward(z, 0, early, pot_hbm)
    load_coup.start()
    load_rowb.start()
    cross, beside = others[:half], others[half:]

    def near_load(row):
        return pltpu.make_async_copy(near_hbm.at[row, 0], near.at[row], near_sem.at[row])

    for target in others + [z]:
        for j in range(owned):
            near_load(target * owned + j).start()
    load_inj.start()
    load_inv.start()
    load_pot.wait()
    load_colb.wait()

    pot = group[pl.ds(z * owned, owned)].reshape(owned * scen, panels)
    basis = colb[...].reshape(width, panels)
    products = lax.dot_general(
        pot,
        jnp.concatenate([basis] * (128 // width), axis=0),
        NT,
        preferred_element_type=jnp.float32,
    )
    lane = lax.broadcasted_iota(jnp.int32, (scen, 128), 1)
    inner = lane % width
    here = (lane // width) == p % (128 // width)
    mine_coef = jnp.zeros((scen, 128), jnp.float32)
    for j in range(owned):
        keep = here & (inner // rank_cap == j) & (inner % rank_cap < ranks_ref[j])
        mine_coef = jnp.where(keep, products[j * scen : (j + 1) * scen], mine_coef)
    coef[p] = mine_coef.astype(jnp.bfloat16)
    coef_copies = []
    for e in range(1, n_prod):
        coef_copies.append(
            pltpu.make_async_remote_copy(
                src_ref=coef.at[p],
                dst_ref=coef.at[p],
                send_sem=coef_send.at[e],
                recv_sem=coef_recv.at[p],
                device_id=((p + e) % n_prod, z),
                device_id_type=MESH,
            )
        )
        coef_copies[-1].start()

    def collect(index):
        zs = nearest[index]
        pltpu.make_async_remote_copy(
            src_ref=slot(zs),
            dst_ref=slot(zs),
            send_sem=gather_send.at[0],
            recv_sem=gather_recv.at[zs],
            device_id=(p, zs),
            device_id_type=MESH,
        ).wait_recv()
        forward(zs, index + 1, early if index < half - 1 else later)

    for index in range(half - 1):
        collect(index)

    for e in range(1, n_prod):
        b = (p + e) % n_prod
        pltpu.make_async_remote_copy(
            src_ref=coef.at[b],
            dst_ref=coef.at[b],
            send_sem=coef_send.at[0],
            recv_sem=coef_recv.at[b],
            device_id=(b, z),
            device_id_type=MESH,
        ).wait_recv()
    load_coup.wait()
    load_rowb.wait()
    share = 128 // width
    blocks = []
    for m in range(n_prod // share):
        block = coef[m * share]
        for e in range(1, share):
            block = block + coef[m * share + e]
        blocks.append(block)
    columns = jnp.concatenate(blocks, axis=1)
    weights = lax.dot_general(
        columns,
        coup[...].reshape(rows * rank_cap, n_prod * width),
        NT,
        preferred_element_type=jnp.float32,
    )
    weights = jnp.concatenate([weights] * rows, axis=0)
    shape = (rows * scen, rows * rank_cap)
    row_of = lax.broadcasted_iota(jnp.int32, shape, 0) // scen
    col_of = lax.broadcasted_iota(jnp.int32, shape, 1) // rank_cap
    weights = jnp.where(row_of == col_of, weights, 0.0).astype(jnp.bfloat16)
    far[...] = jnp.dot(
        weights,
        rowb[...].reshape(rows * rank_cap, panels),
        preferred_element_type=jnp.float32,
    ).reshape(rows, scen, panels)

    offset = p * rows

    def partial_row(row, buffer, upper):
        index = cols_ref[row] - offset
        beyond = jnp.where(upper == 1, index - rows, index + half_rows)
        outside = (index < 0) | (index >= rows)
        picked = jnp.where(
            outside,
            buffer[jnp.clip(beyond, 0, half_rows - 1)],
            group[jnp.clip(index, 0, rows - 1)],
        )
        value = lax.dot_general(picked, near[row], NT, preferred_element_type=jnp.float32)
        return value + far[row]

    def part_copy(target):
        return pltpu.make_async_remote_copy(
            src_ref=sending.at[target],
            dst_ref=arriving.at[z],
            send_sem=part_send.at[target],
            recv_sem=part_recv.at[z],
            device_id=(p, target),
            device_id_type=MESH,
        )

    def rows_of(target, buffer, upper):
        return [partial_row(target * owned + j, buffer, upper) for j in range(owned)]

    def send_rows(targets, buffer, upper):
        for target in targets:
            for j, value in enumerate(rows_of(target, buffer, upper)):
                sending[target, j] = value.astype(jnp.bfloat16)
            part_copy(target).start()

    def keep_rows(buffer, upper):
        for j, value in enumerate(rows_of(z, buffer, upper)):
            mine[j] = inj[j] - value

    for row in range(rows):
        near_load(row).wait()
    load_inj.wait()
    load_inv.wait()
    for index in range(half - 1, n_pre - 1):
        collect(index)
    await_halo(early, 1 - high)
    send_rows(cross, early, 1 - high)
    await_halo(later, high)
    send_rows(beside, later, high)
    keep_rows(later, high)
    for zs in nearest:
        pltpu.make_async_remote_copy(
            src_ref=arriving.at[zs],
            dst_ref=arriving.at[zs],
            send_sem=part_send.at[zs],
            recv_sem=part_recv.at[zs],
            device_id=(p, zs),
            device_id_type=MESH,
        ).wait_recv()
    residual = mine[...]
    for zs in nearest:
        residual = residual - arriving[zs].astype(jnp.float32)
    res_ref[...] = residual
    rounded = residual.astype(jnp.bfloat16)
    for j in range(owned):
        cor_ref[j] = lax.dot_general(
            rounded[j], inv[j], NT, preferred_element_type=jnp.float32
        )
    parts = [part_copy(target) for target in others]
    for copy in gathers + coef_copies + parts:
        copy.wait_send()
    for ok, copy in halos:

        @pl.when(ok)
        def _():
            copy.wait_send()


def hand_over(res_in, cor_in, res_out, cor_out, sem):
    stores = [
        pltpu.make_async_copy(res_in, res_out, sem.at[0]),
        pltpu.make_async_copy(cor_in, cor_out, sem.at[1]),
    ]
    for copy in stores:
        copy.start()
    for copy in stores:
        copy.wait()


def local(n_prod, n_pre, potentials, injected, near, cols, rowb, colb, ranks, coup, inv):
    owned, scen, panels = potentials.shape
    rows = near.shape[0]
    out = jax.ShapeDtypeStruct(injected.shape, jnp.float32)
    anywhere = pl.BlockSpec(memory_space=pltpu.HBM)
    vmem = pl.BlockSpec(memory_space=pltpu.VMEM)
    held = pltpu.VMEM(injected.shape, jnp.float32)
    scalars = pl.BlockSpec(memory_space=pltpu.SMEM)
    dma = pltpu.SemaphoreType.DMA
    blocks = rows + owned
    residual, corrected = pl.pallas_call(
        functools.partial(kernel, n_prod, n_pre),
        out_shape=(held, held),
        in_specs=[
            anywhere,
            anywhere,
            anywhere,
            scalars,
            anywhere,
            anywhere,
            scalars,
            anywhere,
            anywhere,
        ],
        out_specs=(vmem, vmem),
        scratch_shapes=[
            pltpu.VMEM((rows, scen, panels), jnp.bfloat16),
            pltpu.VMEM((rows // 2, scen, panels), jnp.bfloat16),
            pltpu.VMEM((rows // 2, scen, panels), jnp.bfloat16),
            pltpu.VMEM(injected.shape, jnp.float32),
            pltpu.VMEM((rows, panels, panels), jnp.bfloat16),
            pltpu.VMEM(rowb.shape, jnp.bfloat16),
            pltpu.VMEM(colb.shape, jnp.bfloat16),
            pltpu.VMEM(coup.shape, jnp.bfloat16),
            pltpu.VMEM(inv.shape, jnp.bfloat16),
            pltpu.VMEM((n_prod, scen, 128), jnp.bfloat16),
            pltpu.VMEM((rows, scen, panels), jnp.float32),
            pltpu.VMEM(injected.shape, jnp.float32),
            pltpu.VMEM((n_pre, owned, scen, panels), jnp.bfloat16),
            pltpu.VMEM((n_pre, owned, scen, panels), jnp.bfloat16),
            dma((6,)),
            dma((rows,)),
            dma((n_pre,)),
            dma((n_pre,)),
            dma((n_pre,)),
            dma((n_pre,)),
            dma((n_prod,)),
            dma((n_prod,)),
            dma((n_pre,)),
            dma((n_pre,)),
        ],
        compiler_params=pltpu.CompilerParams(
            collective_id=0, has_side_effects=True, vmem_limit_bytes=63 * 2**20
        ),
        cost_estimate=pl.CostEstimate(
            flops=2 * blocks * scen * panels * panels,
            bytes_accessed=2 * blocks * panels * panels,
            transcendentals=0,
        ),
    )(potentials, injected, near, cols.reshape(rows), rowb, colb, ranks, coup, inv)
    return pl.pallas_call(
        hand_over,
        out_shape=(out, out),
        in_specs=[vmem, vmem],
        out_specs=(anywhere, anywhere),
        scratch_shapes=[dma((2,))],
        compiler_params=pltpu.CompilerParams(vmem_limit_bytes=8 * 2**20),
    )(residual, corrected)


def solution(mesh):
    return jax.shard_map(
        functools.partial(local, mesh.shape["prod"], mesh.shape["pre"]),
        mesh=mesh,
        in_specs=(
            P(("prod", "pre"), None, None),
            P(("prod", "pre"), None, None),
            P("prod", "pre", None, None),
            P("prod", "pre"),
            P("prod", None, None),
            P(("prod", "pre"), None, None),
            P(("prod", "pre")),
            P("prod", None, "pre"),
            P(("prod", "pre"), None, None),
        ),
        out_specs=(P(("prod", "pre"), None, None), P(("prod", "pre"), None, None)),
        check_vma=False,
    )
```

```python
import functools

import jax
import jax.numpy as jnp
from jax import lax
from jax.experimental import pallas as pl
from jax.experimental.pallas import tpu as pltpu
from jax.sharding import PartitionSpec as P

MESH = pl.DeviceIdType.MESH
NT = (((1,), (1,)), ((), ()))


def kernel(
    n_prod,
    n_pre,
    pot_hbm,
    inj_hbm,
    near_hbm,
    cols_ref,
    rowb_hbm,
    colb_hbm,
    ranks_ref,
    coup_hbm,
    inv_hbm,
    res_ref,
    cor_ref,
    group,
    early,
    later,
    inj,
    near,
    rowb,
    colb,
    coup,
    inv,
    coef,
    far,
    mine,
    sending,
    arriving,
    load_sem,
    near_sem,
    gather_send,
    gather_recv,
    halo_send,
    halo_recv,
    coef_send,
    coef_recv,
    part_send,
    part_recv,
):
    owned, scen, panels = pot_hbm.shape
    rows = near_hbm.shape[0]
    rank_cap = colb_hbm.shape[1]
    half_rows = rows // 2
    half = n_pre // 2
    width = owned * rank_cap
    p = lax.axis_index("prod")
    z = lax.axis_index("pre")
    high, low = z // half, z % half
    others = [(1 - high) * half + (low + e) % half for e in range(half)]
    others += [high * half + (low + e) % half for e in range(1, half)]
    nearest = others[half:] + others[:half]

    def slot(first):
        return group.at[pl.ds(first * owned, owned)]

    load_pot = pltpu.make_async_copy(pot_hbm, slot(z), load_sem.at[0])
    load_colb = pltpu.make_async_copy(colb_hbm, colb, load_sem.at[1])
    load_coup = pltpu.make_async_copy(coup_hbm, coup, load_sem.at[2])
    load_rowb = pltpu.make_async_copy(rowb_hbm, rowb, load_sem.at[3])
    load_inj = pltpu.make_async_copy(inj_hbm, inj, load_sem.at[4])
    load_inv = pltpu.make_async_copy(inv_hbm, inv, load_sem.at[5])
    load_pot.start()
    load_colb.start()

    barrier = pltpu.get_barrier_semaphore()
    for target in others:
        pl.semaphore_signal(barrier, inc=1, device_id=(p, target), device_id_type=MESH)
    for e in range(1, n_prod):
        pl.semaphore_signal(
            barrier, inc=1, device_id=((p + e) % n_prod, z), device_id_type=MESH
        )
    pl.semaphore_wait(barrier, n_pre - 1 + n_prod - 1)

    gathers = []
    for e, target in enumerate(others):
        gathers.append(
            pltpu.make_async_remote_copy(
                src_ref=pot_hbm,
                dst_ref=slot(z),
                send_sem=gather_send.at[e],
                recv_sem=gather_recv.at[z],
                device_id=(p, target),
                device_id_type=MESH,
            )
        )
        gathers[-1].start()

    halos = []

    def halo_copy(buffer, zs, send, source, to):
        return pltpu.make_async_remote_copy(
            src_ref=source,
            dst_ref=buffer.at[pl.ds(zs % half * owned, owned)],
            send_sem=halo_send.at[send],
            recv_sem=halo_recv.at[zs],
            device_id=(to, z),
            device_id_type=MESH,
        )

    def forward(zs, index, buffer, source=None):
        source = slot(zs) if source is None else source
        to = jnp.where(zs < half, p - 1, p + 1)
        ok = (z >= 1) & (to >= 0) & (to < n_prod)
        copy = halo_copy(buffer, zs, index, source, to)

        @pl.when(ok)
        def _():
            copy.start()

        halos.append((ok, copy))

    def await_halo(buffer, upper):
        source = p - 1 + 2 * upper

        @pl.when((z >= 1) & (source >= 0) & (source < n_prod))
        def _():
            for e in range(half):
                zs = (1 - upper) * half + e
                halo_copy(buffer, zs, 0, slot(zs), source).wait_recv()

    forward(z, 0, early, pot_hbm)
    load_coup.start()
    load_rowb.start()
    cross, beside = others[:half], others[half:]

    def near_load(row):
        return pltpu.make_async_copy(near_hbm.at[row, 0], near.at[row], near_sem.at[row])

    for target in others + [z]:
        for j in range(owned):
            near_load(target * owned + j).start()
    load_inj.start()
    load_inv.start()
    load_pot.wait()
    load_colb.wait()

    pot = group[pl.ds(z * owned, owned)].reshape(owned * scen, panels)
    basis = colb[...].reshape(width, panels)
    products = lax.dot_general(
        pot,
        jnp.concatenate([basis] * (128 // width), axis=0),
        NT,
        preferred_element_type=jnp.float32,
    )
    lane = lax.broadcasted_iota(jnp.int32, (scen, 128), 1)
    inner = lane % width
    here = (lane // width) == p % (128 // width)
    mine_coef = jnp.zeros((scen, 128), jnp.float32)
    for j in range(owned):
        keep = here & (inner // rank_cap == j) & (inner % rank_cap < ranks_ref[j])
        mine_coef = jnp.where(keep, products[j * scen : (j + 1) * scen], mine_coef)
    coef[p] = mine_coef.astype(jnp.bfloat16)
    coef_copies = []
    for e in range(1, n_prod):
        coef_copies.append(
            pltpu.make_async_remote_copy(
                src_ref=coef.at[p],
                dst_ref=coef.at[p],
                send_sem=coef_send.at[e],
                recv_sem=coef_recv.at[p],
                device_id=((p + e) % n_prod, z),
                device_id_type=MESH,
            )
        )
        coef_copies[-1].start()

    def collect(index):
        zs = nearest[index]
        pltpu.make_async_remote_copy(
            src_ref=slot(zs),
            dst_ref=slot(zs),
            send_sem=gather_send.at[0],
            recv_sem=gather_recv.at[zs],
            device_id=(p, zs),
            device_id_type=MESH,
        ).wait_recv()
        forward(zs, index + 1, early if index < half - 1 else later)

    for index in range(n_pre - 1):
        collect(index)

    for e in range(1, n_prod):
        b = (p + e) % n_prod
        pltpu.make_async_remote_copy(
            src_ref=coef.at[b],
            dst_ref=coef.at[b],
            send_sem=coef_send.at[0],
            recv_sem=coef_recv.at[b],
            device_id=(b, z),
            device_id_type=MESH,
        ).wait_recv()
    load_coup.wait()
    load_rowb.wait()
    share = 128 // width
    blocks = []
    for m in range(n_prod // share):
        block = coef[m * share]
        for e in range(1, share):
            block = block + coef[m * share + e]
        blocks.append(block)
    columns = jnp.concatenate(blocks, axis=1)
    weights = lax.dot_general(
        columns,
        coup[...].reshape(rows * rank_cap, n_prod * width),
        NT,
        preferred_element_type=jnp.float32,
    )
    weights = jnp.concatenate([weights] * rows, axis=0)
    shape = (rows * scen, rows * rank_cap)
    row_of = lax.broadcasted_iota(jnp.int32, shape, 0) // scen
    col_of = lax.broadcasted_iota(jnp.int32, shape, 1) // rank_cap
    weights = jnp.where(row_of == col_of, weights, 0.0).astype(jnp.bfloat16)
    far[...] = jnp.dot(
        weights,
        rowb[...].reshape(rows * rank_cap, panels),
        preferred_element_type=jnp.float32,
    ).reshape(rows, scen, panels)

    offset = p * rows

    def partial_row(row, buffer, upper):
        index = cols_ref[row] - offset
        beyond = jnp.where(upper == 1, index - rows, index + half_rows)
        outside = (index < 0) | (index >= rows)
        picked = jnp.where(
            outside,
            buffer[jnp.clip(beyond, 0, half_rows - 1)],
            group[jnp.clip(index, 0, rows - 1)],
        )
        value = lax.dot_general(picked, near[row], NT, preferred_element_type=jnp.float32)
        return value + far[row]

    def part_copy(target):
        return pltpu.make_async_remote_copy(
            src_ref=sending.at[target],
            dst_ref=arriving.at[z],
            send_sem=part_send.at[target],
            recv_sem=part_recv.at[z],
            device_id=(p, target),
            device_id_type=MESH,
        )

    def rows_of(target, buffer, upper):
        return [partial_row(target * owned + j, buffer, upper) for j in range(owned)]

    def send_rows(targets, buffer, upper):
        for target in targets:
            for j, value in enumerate(rows_of(target, buffer, upper)):
                sending[target, j] = value.astype(jnp.bfloat16)
            part_copy(target).start()

    def keep_rows(buffer, upper):
        for j, value in enumerate(rows_of(z, buffer, upper)):
            mine[j] = inj[j] - value

    for row in range(rows):
        near_load(row).wait()
    load_inj.wait()
    load_inv.wait()
    await_halo(early, 1 - high)
    send_rows(cross, early, 1 - high)
    await_halo(later, high)
    send_rows(beside, later, high)
    keep_rows(later, high)
    for zs in nearest:
        pltpu.make_async_remote_copy(
            src_ref=arriving.at[zs],
            dst_ref=arriving.at[zs],
            send_sem=part_send.at[zs],
            recv_sem=part_recv.at[zs],
            device_id=(p, zs),
            device_id_type=MESH,
        ).wait_recv()
    residual = mine[...]
    for zs in nearest:
        residual = residual - arriving[zs].astype(jnp.float32)
    res_ref[...] = residual
    rounded = residual.astype(jnp.bfloat16)
    for j in range(owned):
        cor_ref[j] = lax.dot_general(
            rounded[j], inv[j], NT, preferred_element_type=jnp.float32
        )
    parts = [part_copy(target) for target in others]
    for copy in gathers + coef_copies + parts:
        copy.wait_send()
    for ok, copy in halos:

        @pl.when(ok)
        def _():
            copy.wait_send()


def hand_over(res_in, cor_in, res_out, cor_out, sem):
    stores = [
        pltpu.make_async_copy(res_in, res_out, sem.at[0]),
        pltpu.make_async_copy(cor_in, cor_out, sem.at[1]),
    ]
    for copy in stores:
        copy.start()
    for copy in stores:
        copy.wait()


def local(n_prod, n_pre, potentials, injected, near, cols, rowb, colb, ranks, coup, inv):
    owned, scen, panels = potentials.shape
    rows = near.shape[0]
    out = jax.ShapeDtypeStruct(injected.shape, jnp.float32)
    anywhere = pl.BlockSpec(memory_space=pltpu.HBM)
    vmem = pl.BlockSpec(memory_space=pltpu.VMEM)
    held = pltpu.VMEM(injected.shape, jnp.float32)
    scalars = pl.BlockSpec(memory_space=pltpu.SMEM)
    dma = pltpu.SemaphoreType.DMA
    blocks = rows + owned
    residual, corrected = pl.pallas_call(
        functools.partial(kernel, n_prod, n_pre),
        out_shape=(held, held),
        in_specs=[
            anywhere,
            anywhere,
            anywhere,
            scalars,
            anywhere,
            anywhere,
            scalars,
            anywhere,
            anywhere,
        ],
        out_specs=(vmem, vmem),
        scratch_shapes=[
            pltpu.VMEM((rows, scen, panels), jnp.bfloat16),
            pltpu.VMEM((rows // 2, scen, panels), jnp.bfloat16),
            pltpu.VMEM((rows // 2, scen, panels), jnp.bfloat16),
            pltpu.VMEM(injected.shape, jnp.float32),
            pltpu.VMEM((rows, panels, panels), jnp.bfloat16),
            pltpu.VMEM(rowb.shape, jnp.bfloat16),
            pltpu.VMEM(colb.shape, jnp.bfloat16),
            pltpu.VMEM(coup.shape, jnp.bfloat16),
            pltpu.VMEM(inv.shape, jnp.bfloat16),
            pltpu.VMEM((n_prod, scen, 128), jnp.bfloat16),
            pltpu.VMEM((rows, scen, panels), jnp.float32),
            pltpu.VMEM(injected.shape, jnp.float32),
            pltpu.VMEM((n_pre, owned, scen, panels), jnp.bfloat16),
            pltpu.VMEM((n_pre, owned, scen, panels), jnp.bfloat16),
            dma((6,)),
            dma((rows,)),
            dma((n_pre,)),
            dma((n_pre,)),
            dma((n_pre,)),
            dma((n_pre,)),
            dma((n_prod,)),
            dma((n_prod,)),
            dma((n_pre,)),
            dma((n_pre,)),
        ],
        compiler_params=pltpu.CompilerParams(
            collective_id=0, has_side_effects=True, vmem_limit_bytes=63 * 2**20
        ),
        cost_estimate=pl.CostEstimate(
            flops=2 * blocks * scen * panels * panels,
            bytes_accessed=2 * blocks * panels * panels,
            transcendentals=0,
        ),
    )(potentials, injected, near, cols.reshape(rows), rowb, colb, ranks, coup, inv)
    return pl.pallas_call(
        hand_over,
        out_shape=(out, out),
        in_specs=[vmem, vmem],
        out_specs=(anywhere, anywhere),
        scratch_shapes=[dma((2,))],
        compiler_params=pltpu.CompilerParams(vmem_limit_bytes=8 * 2**20),
    )(residual, corrected)


def solution(mesh):
    return jax.shard_map(
        functools.partial(local, mesh.shape["prod"], mesh.shape["pre"]),
        mesh=mesh,
        in_specs=(
            P(("prod", "pre"), None, None),
            P(("prod", "pre"), None, None),
            P("prod", "pre", None, None),
            P("prod", "pre"),
            P("prod", None, None),
            P(("prod", "pre"), None, None),
            P(("prod", "pre")),
            P("prod", None, "pre"),
            P(("prod", "pre"), None, None),
        ),
        out_specs=(P(("prod", "pre"), None, None), P(("prod", "pre"), None, None)),
        check_vma=False,
    )
```

```python
import functools

import jax
import jax.numpy as jnp
from jax import lax
from jax.experimental import pallas as pl
from jax.experimental.pallas import tpu as pltpu
from jax.sharding import PartitionSpec as P

MESH = pl.DeviceIdType.MESH
NT = (((1,), (1,)), ((), ()))


def kernel(
    n_prod,
    n_pre,
    pot_hbm,
    inj_hbm,
    near_hbm,
    cols_ref,
    rowb_hbm,
    colb_hbm,
    ranks_ref,
    coup_hbm,
    inv_hbm,
    res_ref,
    cor_ref,
    group,
    early,
    later,
    inj,
    near,
    rowb,
    colb,
    coup,
    inv,
    coef,
    far,
    mine,
    sending,
    arriving,
    load_sem,
    near_sem,
    gather_send,
    gather_recv,
    halo_send,
    halo_recv,
    coef_send,
    coef_recv,
    part_send,
    part_recv,
):
    owned, scen, panels = pot_hbm.shape
    rows = near_hbm.shape[0]
    rank_cap = colb_hbm.shape[1]
    half_rows = rows // 2
    half = n_pre // 2
    width = owned * rank_cap
    p = lax.axis_index("prod")
    z = lax.axis_index("pre")
    high, low = z // half, z % half
    others = [(1 - high) * half + (low + e) % half for e in range(half)]
    others += [high * half + (low + e) % half for e in range(1, half)]
    nearest = others[half:] + others[:half]

    def slot(first):
        return group.at[pl.ds(first * owned, owned)]

    load_pot = pltpu.make_async_copy(pot_hbm, slot(z), load_sem.at[0])
    load_colb = pltpu.make_async_copy(colb_hbm, colb, load_sem.at[1])
    load_coup = pltpu.make_async_copy(coup_hbm, coup, load_sem.at[2])
    load_rowb = pltpu.make_async_copy(rowb_hbm, rowb, load_sem.at[3])
    load_inj = pltpu.make_async_copy(inj_hbm, inj, load_sem.at[4])
    load_inv = pltpu.make_async_copy(inv_hbm, inv, load_sem.at[5])
    load_pot.start()
    load_colb.start()

    barrier = pltpu.get_barrier_semaphore()
    for target in others:
        pl.semaphore_signal(barrier, inc=1, device_id=(p, target), device_id_type=MESH)
    for e in range(1, n_prod):
        pl.semaphore_signal(
            barrier, inc=1, device_id=((p + e) % n_prod, z), device_id_type=MESH
        )
    load_pot.wait()
    load_colb.wait()
    pot = group[pl.ds(z * owned, owned)].reshape(owned * scen, panels)
    basis = colb[...].reshape(width, panels)
    products = lax.dot_general(
        pot,
        jnp.concatenate([basis] * (128 // width), axis=0),
        NT,
        preferred_element_type=jnp.float32,
    )
    lane = lax.broadcasted_iota(jnp.int32, (scen, 128), 1)
    inner = lane % width
    here = (lane // width) == p % (128 // width)
    mine_coef = jnp.zeros((scen, 128), jnp.float32)
    for j in range(owned):
        keep = here & (inner // rank_cap == j) & (inner % rank_cap < ranks_ref[j])
        mine_coef = jnp.where(keep, products[j * scen : (j + 1) * scen], mine_coef)
    coef[p] = mine_coef.astype(jnp.bfloat16)
    pl.semaphore_wait(barrier, n_pre - 1 + n_prod - 1)
    coef_copies = []
    for e in range(1, n_prod):
        coef_copies.append(
            pltpu.make_async_remote_copy(
                src_ref=coef.at[p],
                dst_ref=coef.at[p],
                send_sem=coef_send.at[e],
                recv_sem=coef_recv.at[p],
                device_id=((p + e) % n_prod, z),
                device_id_type=MESH,
            )
        )
        coef_copies[-1].start()


    gathers = []
    for e, target in enumerate(others):
        gathers.append(
            pltpu.make_async_remote_copy(
                src_ref=pot_hbm,
                dst_ref=slot(z),
                send_sem=gather_send.at[e],
                recv_sem=gather_recv.at[z],
                device_id=(p, target),
                device_id_type=MESH,
            )
        )
        gathers[-1].start()

    halos = []

    def halo_copy(buffer, zs, send, source, to):
        return pltpu.make_async_remote_copy(
            src_ref=source,
            dst_ref=buffer.at[pl.ds(zs % half * owned, owned)],
            send_sem=halo_send.at[send],
            recv_sem=halo_recv.at[zs],
            device_id=(to, z),
            device_id_type=MESH,
        )

    def forward(zs, index, buffer, source=None):
        source = slot(zs) if source is None else source
        to = jnp.where(zs < half, p - 1, p + 1)
        ok = (z >= 1) & (to >= 0) & (to < n_prod)
        copy = halo_copy(buffer, zs, index, source, to)

        @pl.when(ok)
        def _():
            copy.start()

        halos.append((ok, copy))

    def await_halo(buffer, upper):
        source = p - 1 + 2 * upper

        @pl.when((z >= 1) & (source >= 0) & (source < n_prod))
        def _():
            for e in range(half):
                zs = (1 - upper) * half + e
                halo_copy(buffer, zs, 0, slot(zs), source).wait_recv()

    forward(z, 0, early, pot_hbm)
    load_coup.start()
    load_rowb.start()
    cross, beside = others[:half], others[half:]

    def near_load(row):
        return pltpu.make_async_copy(near_hbm.at[row, 0], near.at[row], near_sem.at[row])

    for target in others + [z]:
        for j in range(owned):
            near_load(target * owned + j).start()
    load_inj.start()
    load_inv.start()

    def collect(index):
        zs = nearest[index]
        pltpu.make_async_remote_copy(
            src_ref=slot(zs),
            dst_ref=slot(zs),
            send_sem=gather_send.at[0],
            recv_sem=gather_recv.at[zs],
            device_id=(p, zs),
            device_id_type=MESH,
        ).wait_recv()
        forward(zs, index + 1, early if index < half - 1 else later)

    for index in range(half - 1):
        collect(index)

    for e in range(1, n_prod):
        b = (p + e) % n_prod
        pltpu.make_async_remote_copy(
            src_ref=coef.at[b],
            dst_ref=coef.at[b],
            send_sem=coef_send.at[0],
            recv_sem=coef_recv.at[b],
            device_id=(b, z),
            device_id_type=MESH,
        ).wait_recv()
    load_coup.wait()
    load_rowb.wait()
    share = 128 // width
    blocks = []
    for m in range(n_prod // share):
        block = coef[m * share]
        for e in range(1, share):
            block = block + coef[m * share + e]
        blocks.append(block)
    columns = jnp.concatenate(blocks, axis=1)
    weights = lax.dot_general(
        columns,
        coup[...].reshape(rows * rank_cap, n_prod * width),
        NT,
        preferred_element_type=jnp.float32,
    )
    weights = jnp.concatenate([weights] * rows, axis=0)
    shape = (rows * scen, rows * rank_cap)
    row_of = lax.broadcasted_iota(jnp.int32, shape, 0) // scen
    col_of = lax.broadcasted_iota(jnp.int32, shape, 1) // rank_cap
    weights = jnp.where(row_of == col_of, weights, 0.0).astype(jnp.bfloat16)
    far[...] = jnp.dot(
        weights,
        rowb[...].reshape(rows * rank_cap, panels),
        preferred_element_type=jnp.float32,
    ).reshape(rows, scen, panels)

    offset = p * rows

    def partial_row(row, buffer, upper):
        index = cols_ref[row] - offset
        beyond = jnp.where(upper == 1, index - rows, index + half_rows)
        outside = (index < 0) | (index >= rows)
        picked = jnp.where(
            outside,
            buffer[jnp.clip(beyond, 0, half_rows - 1)],
            group[jnp.clip(index, 0, rows - 1)],
        )
        value = lax.dot_general(picked, near[row], NT, preferred_element_type=jnp.float32)
        return value + far[row]

    def part_copy(target):
        return pltpu.make_async_remote_copy(
            src_ref=sending.at[target],
            dst_ref=arriving.at[z],
            send_sem=part_send.at[target],
            recv_sem=part_recv.at[z],
            device_id=(p, target),
            device_id_type=MESH,
        )

    def rows_of(target, buffer, upper):
        return [partial_row(target * owned + j, buffer, upper) for j in range(owned)]

    def send_rows(targets, buffer, upper):
        for target in targets:
            for j, value in enumerate(rows_of(target, buffer, upper)):
                sending[target, j] = value.astype(jnp.bfloat16)
            part_copy(target).start()

    def keep_rows(buffer, upper):
        for j, value in enumerate(rows_of(z, buffer, upper)):
            mine[j] = inj[j] - value

    for row in range(rows):
        near_load(row).wait()
    load_inj.wait()
    load_inv.wait()
    for index in range(half - 1, n_pre - 1):
        collect(index)
    await_halo(early, 1 - high)
    send_rows(cross, early, 1 - high)
    await_halo(later, high)
    send_rows(beside, later, high)
    keep_rows(later, high)
    for zs in nearest:
        pltpu.make_async_remote_copy(
            src_ref=arriving.at[zs],
            dst_ref=arriving.at[zs],
            send_sem=part_send.at[zs],
            recv_sem=part_recv.at[zs],
            device_id=(p, zs),
            device_id_type=MESH,
        ).wait_recv()
    residual = mine[...]
    for zs in nearest:
        residual = residual - arriving[zs].astype(jnp.float32)
    res_ref[...] = residual
    rounded = residual.astype(jnp.bfloat16)
    for j in range(owned):
        cor_ref[j] = lax.dot_general(
            rounded[j], inv[j], NT, preferred_element_type=jnp.float32
        )
    parts = [part_copy(target) for target in others]
    for copy in gathers + coef_copies + parts:
        copy.wait_send()
    for ok, copy in halos:

        @pl.when(ok)
        def _():
            copy.wait_send()


def hand_over(res_in, cor_in, res_out, cor_out, sem):
    stores = [
        pltpu.make_async_copy(res_in, res_out, sem.at[0]),
        pltpu.make_async_copy(cor_in, cor_out, sem.at[1]),
    ]
    for copy in stores:
        copy.start()
    for copy in stores:
        copy.wait()


def local(n_prod, n_pre, potentials, injected, near, cols, rowb, colb, ranks, coup, inv):
    owned, scen, panels = potentials.shape
    rows = near.shape[0]
    out = jax.ShapeDtypeStruct(injected.shape, jnp.float32)
    anywhere = pl.BlockSpec(memory_space=pltpu.HBM)
    vmem = pl.BlockSpec(memory_space=pltpu.VMEM)
    held = pltpu.VMEM(injected.shape, jnp.float32)
    scalars = pl.BlockSpec(memory_space=pltpu.SMEM)
    dma = pltpu.SemaphoreType.DMA
    blocks = rows + owned
    residual, corrected = pl.pallas_call(
        functools.partial(kernel, n_prod, n_pre),
        out_shape=(held, held),
        in_specs=[
            anywhere,
            anywhere,
            anywhere,
            scalars,
            anywhere,
            anywhere,
            scalars,
            anywhere,
            anywhere,
        ],
        out_specs=(vmem, vmem),
        scratch_shapes=[
            pltpu.VMEM((rows, scen, panels), jnp.bfloat16),
            pltpu.VMEM((rows // 2, scen, panels), jnp.bfloat16),
            pltpu.VMEM((rows // 2, scen, panels), jnp.bfloat16),
            pltpu.VMEM(injected.shape, jnp.float32),
            pltpu.VMEM((rows, panels, panels), jnp.bfloat16),
            pltpu.VMEM(rowb.shape, jnp.bfloat16),
            pltpu.VMEM(colb.shape, jnp.bfloat16),
            pltpu.VMEM(coup.shape, jnp.bfloat16),
            pltpu.VMEM(inv.shape, jnp.bfloat16),
            pltpu.VMEM((n_prod, scen, 128), jnp.bfloat16),
            pltpu.VMEM((rows, scen, panels), jnp.float32),
            pltpu.VMEM(injected.shape, jnp.float32),
            pltpu.VMEM((n_pre, owned, scen, panels), jnp.bfloat16),
            pltpu.VMEM((n_pre, owned, scen, panels), jnp.bfloat16),
            dma((6,)),
            dma((rows,)),
            dma((n_pre,)),
            dma((n_pre,)),
            dma((n_pre,)),
            dma((n_pre,)),
            dma((n_prod,)),
            dma((n_prod,)),
            dma((n_pre,)),
            dma((n_pre,)),
        ],
        compiler_params=pltpu.CompilerParams(
            collective_id=0, has_side_effects=True, vmem_limit_bytes=63 * 2**20
        ),
        cost_estimate=pl.CostEstimate(
            flops=2 * blocks * scen * panels * panels,
            bytes_accessed=2 * blocks * panels * panels,
            transcendentals=0,
        ),
    )(potentials, injected, near, cols.reshape(rows), rowb, colb, ranks, coup, inv)
    return pl.pallas_call(
        hand_over,
        out_shape=(out, out),
        in_specs=[vmem, vmem],
        out_specs=(anywhere, anywhere),
        scratch_shapes=[dma((2,))],
        compiler_params=pltpu.CompilerParams(vmem_limit_bytes=8 * 2**20),
    )(residual, corrected)


def solution(mesh):
    return jax.shard_map(
        functools.partial(local, mesh.shape["prod"], mesh.shape["pre"]),
        mesh=mesh,
        in_specs=(
            P(("prod", "pre"), None, None),
            P(("prod", "pre"), None, None),
            P("prod", "pre", None, None),
            P("prod", "pre"),
            P("prod", None, None),
            P(("prod", "pre"), None, None),
            P(("prod", "pre")),
            P("prod", None, "pre"),
            P(("prod", "pre"), None, None),
        ),
        out_specs=(P(("prod", "pre"), None, None), P(("prod", "pre"), None, None)),
        check_vma=False,
    )
```
